32 devices in a mesh: req: 4 (over y, x), tp: 8 (over z, core).
Axes of the slice: x: 2, y: 2, z: 4, core: 2. Of those that a mesh axis runs over, the one named last changes fastest.
Arguments:
- step_inputs: bfloat16 [4, 256, 1536], P(None, ('req', 'tp')), may hold values from -6 to 6
- qkv_weight: bfloat16 [1536, 2048], replicated, may hold values from -0.15625 to 0.15625
- qkv_bias: float32 [2048], replicated, may hold values from -8 to 8
- out_weight: bfloat16 [1536, 1536], P('tp'), may hold values from -0.15625 to 0.15625
- gate_weight: bfloat16 [1536, 8960], P(None, 'tp'), may hold values from -0.15625 to 0.15625
- up_weight: bfloat16 [1536, 8960], P(None, 'tp'), may hold values from -0.15625 to 0.15625
- down_weight: bfloat16 [8960, 1536], P('tp'), may hold values from -0.0625 to 0.0625
- cache_keys: bfloat16 [256, 4096, 256], P(('req', 'tp')), may hold values from -60 to 60
- cache_values: bfloat16 [256, 4096, 256], P(('req', 'tp')), may hold values from -24 to 24
- lengths: int32 [32, 8], replicated, may hold values from 1 to 4096, as said below
- parents: int32 [4, 32, 8], replicated, may hold values from 0 to 7
- slot_request: int32 [32], replicated, may hold values from 0 to 31, each once
Outputs:
- outputs: bfloat16 [4, 256, 1536], P(None, ('req', 'tp'))
The draws below stay inside these ranges and needn't reach their ends.
Inputs may be any that keep to these rules, and one draw needn't show every extreme that they name: lengths[r, c] is the number of cached positions of beam c of request r; some beam has exactly 4096. parents[t, r, b] names a beam of the same request r. `slot_request`: a permutation of the requests; slots 8 * i to 8 * i + 7 are rows of index i of req.
All inputs are finite; a program needn't handle non-finite values.
Results may differ from the reference program's by a relative error of at most 0.022.
The reference program's roundings to bfloat16 on the way count: a program that leaves them out, or rounds other values in their place, can miss the bound.
Values may be sent and summed in bfloat16 or wider, within the bound.
A program may use at most 192 MiB of HBM per device.

```python
import jax
import jax.numpy as jnp
from jax import lax

D = 1536
Q_HEADS = 12
KV_HEADS = 2
HEAD_DIM = 128
FF = 8960
BEAMS = 8
STEPS = 4
LEN = 4096
REQUESTS = 32
ATTN_WIDTH = 1536
KV_WIDTH = 256
QKV = 2048


def draw_cache_keys(key, part):
    shape = (REQUESTS * BEAMS, LEN, KV_HEADS * HEAD_DIM)
    values = jnp.clip(2.5 * jax.random.normal(key, shape, jnp.float32), -15.0, 15.0)
    return values.astype(jnp.bfloat16)


def draw_qkv_bias(key, part):
    total = (Q_HEADS + 2 * KV_HEADS) * HEAD_DIM
    noise = jax.random.normal(key, (total,), jnp.float32)
    values = 0.5 * noise
    return jnp.clip(values, -8.0, 8.0)


def draw_lengths(key, part):
    values = jax.random.randint(key, (REQUESTS, BEAMS), 1, LEN + 1, dtype=jnp.int32)
    return values.at[0, 0].set(LEN)


def place_ends(drawn, stream_key, smallest, top_value):
    spot = [jax.random.randint(jax.random.fold_in(stream_key, axis), (), 0, length) for axis, length in enumerate(drawn.shape)]
    longest = drawn.shape.index(max(drawn.shape))
    beside = spot[:longest] + [(spot[longest] + 1) % drawn.shape[longest]] + spot[longest + 1:]
    return drawn.at[tuple(spot)].set(smallest).at[tuple(beside)].set(top_value)


def block_scale(stream_key, shape, cuts, least, high):
    def one(position, shards_of):
        steps = jax.random.uniform(jax.random.fold_in(jax.random.fold_in(stream_key, 6), position), (shards_of,), jnp.float32, least / len(cuts), high / len(cuts))
        return jnp.repeat(jnp.exp(steps), shape[position] // shards_of).reshape((-1,) + (1,) * (len(shape) - position - 1))

    gain = one(*cuts[0])
    for cut in cuts[1:]:
        gain = gain * one(*cut)
    return gain


def centred(own_key, extent, scale, bound, split=(), held_as=jnp.bfloat16):
    result = jax.random.normal(own_key, extent, jnp.float32) * scale
    if len(split) > 0:
        result = block_scale(own_key, extent, split, -0.22, 0.18) * result
    return jnp.clip(result, min=-bound, max=bound).astype(held_as)


def setup_inputs(seed: int = 0) -> dict:
    key_list = jax.random.split(jax.random.key(seed), 13)
    return {
        "step_inputs": centred(key_list[0], (STEPS, REQUESTS * BEAMS, D), 1.0, 6.0, ((1, 32),)),
        "qkv_weight": centred(key_list[1], (D, QKV), D ** -0.5, 0.15625),
        "qkv_bias": draw_qkv_bias(jax.random.fold_in(key_list[12], 71), 0),
        "out_weight": centred(key_list[3], (ATTN_WIDTH, D), ATTN_WIDTH ** -0.5, 0.15625, ((0, 8),)),
        "gate_weight": centred(key_list[4], (D, FF), D ** -0.5, 0.15625, ((1, 8),)),
        "up_weight": centred(key_list[5], (D, FF), D ** -0.5, 0.15625, ((1, 8),)),
        "down_weight": centred(key_list[6], (FF, D), FF ** -0.5, 0.0625, ((0, 8),)),
        "cache_keys": draw_cache_keys(jax.random.fold_in(key_list[12], 71), 0),
        "cache_values": centred(key_list[8], (REQUESTS * BEAMS, LEN, KV_WIDTH), 4.0, 24.0, ((0, 32),)),
        "lengths": draw_lengths(jax.random.fold_in(key_list[12], 71), 0),
        "parents": place_ends(jax.random.randint(key_list[10], (STEPS, REQUESTS, BEAMS), 0, BEAMS), jax.random.fold_in(key_list[10], 1), 0, BEAMS - 1).astype(jnp.int32),
        "slot_request": jax.random.permutation(key_list[11], REQUESTS).astype(jnp.int32),
    }


theta_base = 1000000.0
norm_eps = 1e-06
masked_score = -1e+30

def rms_normed(values):
    values = values.astype(jnp.float32)
    factor = lax.rsqrt(lax.optimization_barrier(jnp.mean(values * values, axis=-1, keepdims=True)) + norm_eps)
    return (values * factor).astype(jnp.bfloat16)

def rotate(vectors, positions):
    half = vectors.shape[-1] // 2
    freqs = theta_base ** (-jnp.arange(half, dtype=jnp.float32) * 2.0 / vectors.shape[-1])
    angles = positions.astype(jnp.float32)[:, None] * freqs[None, :]
    cosine = jnp.cos(angles)[:, None, :]
    sine = jnp.sin(angles)[:, None, :]
    values = vectors.astype(jnp.float32)
    first = values[..., :half]
    second = values[..., half:]
    return jnp.concatenate([first * cosine - second * sine, second * cosine + first * sine], axis=-1).astype(jnp.bfloat16)

def rounded(values):
    return lax.optimization_barrier(values.astype(jnp.bfloat16)).astype(jnp.float32)

def reference(step_inputs, qkv_weight, qkv_bias, out_weight, gate_weight, up_weight, down_weight, cache_keys, cache_values, lengths, parents, slot_request):
    attn_width = Q_HEADS * HEAD_DIM
    kv_width = KV_HEADS * HEAD_DIM
    group = Q_HEADS // KV_HEADS
    scale = HEAD_DIM ** (-0.5)
    total_rows = REQUESTS * BEAMS
    roots = jnp.broadcast_to(jnp.arange(BEAMS, dtype=jnp.int32)[None, :], (REQUESTS, BEAMS))
    gen_keys = jnp.zeros((STEPS, total_rows, kv_width), jnp.bfloat16)
    gen_values = jnp.zeros((STEPS, total_rows, kv_width), jnp.bfloat16)
    slot_lengths = lengths[slot_request]
    base_rows = (jnp.arange(REQUESTS, dtype=jnp.int32) * BEAMS)[:, None]
    results = []
    for step in range(STEPS):
        roots = jnp.take_along_axis(roots, parents[step], axis=1)
        slot_parents = parents[step][slot_request]
        reorder = (base_rows + slot_parents).reshape(-1)
        gen_keys = jnp.take(gen_keys, reorder, axis=1)
        gen_values = jnp.take(gen_values, reorder, axis=1)
        inputs = step_inputs[step]
        normed = rms_normed(inputs)
        qkv = (jnp.dot(normed, qkv_weight, preferred_element_type=jnp.float32) + qkv_bias).astype(jnp.bfloat16)
        slot_roots = roots[slot_request]
        prefix_lengths = jnp.take_along_axis(slot_lengths, slot_roots, axis=1)
        positions = (prefix_lengths + step).reshape(-1)
        queries = rotate(qkv[:, :attn_width].reshape(total_rows, Q_HEADS, HEAD_DIM), positions)
        new_keys = rotate(qkv[:, attn_width:attn_width + kv_width].reshape(total_rows, KV_HEADS, HEAD_DIM), positions)
        gen_keys = gen_keys.at[step].set(new_keys.reshape(total_rows, kv_width))
        gen_values = gen_values.at[step].set(qkv[:, attn_width + kv_width:])
        cache_rows = slot_request[:, None] * BEAMS + slot_roots
        query_blocks = queries.reshape(REQUESTS, BEAMS, KV_HEADS, group, HEAD_DIM)
        past_keys_all = gen_keys[:step + 1].reshape(step + 1, REQUESTS, BEAMS, KV_HEADS, HEAD_DIM).transpose(1, 0, 2, 3, 4)
        past_values_all = gen_values[:step + 1].reshape(step + 1, REQUESTS, BEAMS, KV_HEADS, HEAD_DIM).transpose(1, 0, 2, 3, 4)

        def one_request(items):
            rows, limits, query_block, past_keys, past_values = items
            keys = jnp.take(cache_keys, rows, axis=0).astype(jnp.float32).reshape(BEAMS, LEN, KV_HEADS, HEAD_DIM)
            values = jnp.take(cache_values, rows, axis=0).astype(jnp.float32).reshape(BEAMS, LEN, KV_HEADS, HEAD_DIM)
            query_block = query_block.astype(jnp.float32)
            prefix_scores = jnp.einsum('bkgd,bpkd->bkgp', query_block, keys) * scale
            live = (jnp.arange(LEN, dtype=jnp.int32)[None, :] < limits[:, None])[:, None, None, :]
            prefix_scores = jnp.where(live, prefix_scores, masked_score)
            recent_scores = jnp.einsum('bkgd,sbkd->bkgs', query_block, past_keys.astype(jnp.float32)) * scale
            top = jnp.maximum(lax.optimization_barrier(jnp.max(prefix_scores, axis=-1)), lax.optimization_barrier(jnp.max(recent_scores, axis=-1)))
            prefix_weights = jnp.where(live, jnp.exp(prefix_scores - top[..., None]), 0.0)
            recent_weights = jnp.exp(recent_scores - top[..., None])
            denominator = lax.optimization_barrier(jnp.sum(prefix_weights, axis=-1)) + lax.optimization_barrier(jnp.sum(recent_weights, axis=-1))
            numerator = jnp.einsum('bkgp,bpkd->bkgd', rounded(prefix_weights), values)
            numerator = numerator + jnp.einsum('bkgs,sbkd->bkgd', rounded(recent_weights), past_values.astype(jnp.float32))
            return (numerator / denominator[..., None]).astype(jnp.bfloat16)
        attention = lax.map(one_request, (cache_rows, prefix_lengths, query_blocks, past_keys_all, past_values_all))
        attention = attention.reshape(total_rows, attn_width)
        middle = inputs.astype(jnp.float32) + jnp.dot(attention, out_weight, preferred_element_type=jnp.float32)
        mixed_in = rms_normed(middle)
        gate = jnp.dot(mixed_in, gate_weight, preferred_element_type=jnp.float32)
        upward = jnp.dot(mixed_in, up_weight, preferred_element_type=jnp.float32)
        hidden = (jax.nn.silu(gate) * upward).astype(jnp.bfloat16)
        results.append((middle + jnp.dot(hidden, down_weight, preferred_element_type=jnp.float32)).astype(jnp.bfloat16))
    return jnp.stack(results)
```

```python
import functools

import jax
import jax.numpy as jnp
from jax import lax
from jax.experimental import pallas as pl
from jax.experimental.pallas import tpu as pltpu
from jax.sharding import PartitionSpec as P

Q_HEADS = 12
KV_HEADS = 2


theta_base = 1000000.0
norm_eps = 1e-06
masked_score = -1e30


def rms_normed(values):
    values = values.astype(jnp.float32)
    factor = lax.rsqrt(jnp.mean(values * values, axis=-1, keepdims=True) + norm_eps)
    return (values * factor).astype(jnp.bfloat16)


def rotate(vectors, positions):
    half = vectors.shape[-1] // 2
    freqs = theta_base ** (-jnp.arange(half, dtype=jnp.float32) * 2.0 / vectors.shape[-1])
    angles = positions.astype(jnp.float32)[:, None] * freqs[None, :]
    cosine = jnp.cos(angles)[:, None, :]
    sine = jnp.sin(angles)[:, None, :]
    values = vectors.astype(jnp.float32)
    first = values[..., :half]
    second = values[..., half:]
    return jnp.concatenate(
        [first * cosine - second * sine, second * cosine + first * sine], axis=-1
    ).astype(jnp.bfloat16)


def owner_rows(flat, owned_count, beams, inverse):
    owned_global = flat * owned_count + jnp.arange(owned_count, dtype=jnp.int32)
    owned_request = owned_global // beams
    owned_beam = owned_global % beams
    beam_range = jnp.arange(beams, dtype=jnp.int32)
    query_rows = (inverse[owned_request][:, None] * beams + beam_range[None, :]).reshape(-1)
    return (owned_request, owned_beam, query_rows)


def owned_attention(
    every_query, keys, values, owned_request, owned_beam, query_rows, root_all, lengths
):
    owned_rows, context, kv_width = keys.shape
    beams = root_all.shape[1]
    head_dim = kv_width // KV_HEADS
    group = Q_HEADS // KV_HEADS
    grouped = jnp.take(every_query, query_rows, axis=0).reshape(
        owned_rows, beams, KV_HEADS, group, head_dim
    )
    keys = keys.reshape(owned_rows, context, KV_HEADS, head_dim)
    values = values.reshape(owned_rows, context, KV_HEADS, head_dim)
    scores = jnp.einsum(
        "jbkgd,jpkd->jbkgp", grouped, keys, preferred_element_type=jnp.float32
    ) * head_dim ** (-0.5)
    limits = lengths[owned_request, owned_beam]
    live = (jnp.arange(context, dtype=jnp.int32)[None, :] < limits[:, None])[:, None, None, None, :]
    scores = jnp.where(live, scores, masked_score)
    peak = jnp.max(scores, axis=-1)
    weights = jnp.where(live, jnp.exp(scores - peak[..., None]), 0.0)
    total = jnp.sum(weights, axis=-1)
    output = jnp.einsum(
        "jbkgp,jpkd->jbkgd",
        weights.astype(jnp.bfloat16),
        values,
        preferred_element_type=jnp.float32,
    )
    chosen = (root_all[owned_request] == owned_beam[:, None])[:, :, None, None]
    peak = jnp.where(chosen, peak, 0.0).reshape(owned_rows * beams, KV_HEADS, group)
    total = jnp.where(chosen, total, 0.0).reshape(owned_rows * beams, KV_HEADS, group)
    output = jnp.where(chosen[..., None], output, 0.0).reshape(
        owned_rows * beams, KV_HEADS, group, head_dim
    )
    return (peak, total, output)


def spread_rows(pieces, target_rows, row_count):
    return tuple(
        (
            jnp.zeros((row_count,) + piece.shape[1:], jnp.float32).at[target_rows].add(piece)
            for piece in pieces
        )
    )


def per_device_split(
    step_inputs,
    qkv_weight,
    qkv_bias,
    out_weight,
    gate_weight,
    up_weight,
    down_weight,
    cache_keys,
    cache_values,
    lengths,
    parents,
    slot_request,
):
    steps_count, rows_dev, width = step_inputs.shape
    beams = parents.shape[2]
    requests = slot_request.shape[0]
    req_count = lax.axis_size("req")
    tp_count = lax.axis_size("tp")
    group_requests = requests // req_count
    group_rows = group_requests * beams
    total_rows = requests * beams
    owned_count = cache_keys.shape[0]
    kv_width = cache_keys.shape[2]
    head_dim = kv_width // KV_HEADS
    group = Q_HEADS // KV_HEADS
    attn_width = Q_HEADS * head_dim
    req_index = lax.axis_index("req")
    tp_index = lax.axis_index("tp")
    flat_index = req_index * tp_count + tp_index
    my_requests = lax.dynamic_slice_in_dim(slot_request, req_index * group_requests, group_requests)
    inverse = (
        jnp.zeros((requests,), jnp.int32)
        .at[slot_request]
        .set(jnp.arange(requests, dtype=jnp.int32))
    )
    owned_request, owned_beam, query_rows = owner_rows(flat_index, owned_count, beams, inverse)
    beam_range = jnp.arange(beams, dtype=jnp.int32)
    root_all = jnp.broadcast_to(beam_range[None, :], (requests, beams))
    gen_keys = jnp.zeros((steps_count, group_rows, kv_width), jnp.bfloat16)
    gen_values = jnp.zeros((steps_count, group_rows, kv_width), jnp.bfloat16)
    base_rows = (jnp.arange(group_requests, dtype=jnp.int32) * beams)[:, None]
    column_width = out_weight.shape[0]
    results = []
    for step in range(steps_count):
        root_all = jnp.take_along_axis(root_all, parents[step], axis=1)
        reorder = (base_rows + parents[step][my_requests]).reshape(-1)
        gen_keys = jnp.take(gen_keys, reorder, axis=1)
        gen_values = jnp.take(gen_values, reorder, axis=1)
        inputs = step_inputs[step]
        normed = rms_normed(inputs)
        qkv = (
            jnp.dot(
                lax.all_gather(normed, "tp", axis=0, tiled=True),
                qkv_weight,
                preferred_element_type=jnp.float32,
            )
            + qkv_bias
        ).astype(jnp.bfloat16)
        my_roots = root_all[my_requests]
        positions = (jnp.take_along_axis(lengths[my_requests], my_roots, axis=1) + step).reshape(-1)
        queries = rotate(qkv[:, :attn_width].reshape(group_rows, Q_HEADS, head_dim), positions)
        new_keys = rotate(
            qkv[:, attn_width : attn_width + kv_width].reshape(group_rows, KV_HEADS, head_dim),
            positions,
        )
        gen_keys = gen_keys.at[step].set(new_keys.reshape(group_rows, kv_width))
        gen_values = gen_values.at[step].set(qkv[:, attn_width + kv_width :])
        every_query = lax.all_gather(
            queries.reshape(group_rows, attn_width), "req", axis=0, tiled=True
        )
        part_peak, part_total, part_output = owned_attention(
            every_query,
            cache_keys,
            cache_values,
            owned_request,
            owned_beam,
            query_rows,
            root_all,
            lengths,
        )
        all_peak, all_total, all_output = spread_rows(
            (part_peak, part_total, part_output), query_rows, total_rows
        )
        sum_peak, sum_total, sum_output = lax.psum((all_peak, all_total, all_output), ("req", "tp"))
        peak = lax.dynamic_slice_in_dim(sum_peak, req_index * group_rows, group_rows, 0)
        total = lax.dynamic_slice_in_dim(sum_total, req_index * group_rows, group_rows, 0)
        output = lax.dynamic_slice_in_dim(sum_output, req_index * group_rows, group_rows, 0)
        grouped = queries.reshape(group_rows, KV_HEADS, group, head_dim)
        past_keys = gen_keys[: step + 1].reshape(step + 1, group_rows, KV_HEADS, head_dim)
        past_values = gen_values[: step + 1].reshape(step + 1, group_rows, KV_HEADS, head_dim)
        recent_scores = jnp.einsum(
            "bkgd,sbkd->bkgs", grouped, past_keys, preferred_element_type=jnp.float32
        ) * head_dim ** (-0.5)
        top = jnp.maximum(peak, jnp.max(recent_scores, axis=-1))
        factor = jnp.exp(peak - top)
        recent_weights = jnp.exp(recent_scores - top[..., None])
        denominator = total * factor + jnp.sum(recent_weights, axis=-1)
        numerator = output * factor[..., None] + jnp.einsum(
            "bkgs,sbkd->bkgd",
            recent_weights.astype(jnp.bfloat16),
            past_values,
            preferred_element_type=jnp.float32,
        )
        attention = (
            (numerator / denominator[..., None])
            .reshape(group_rows, attn_width)
            .astype(jnp.bfloat16)
        )
        columns = lax.dynamic_slice_in_dim(attention, tp_index * column_width, column_width, 1)
        attended = lax.psum_scatter(
            jnp.dot(columns, out_weight, preferred_element_type=jnp.float32).astype(jnp.bfloat16),
            "tp",
            scatter_dimension=0,
            tiled=True,
        ).astype(jnp.float32)
        middle = inputs.astype(jnp.float32) + attended
        mixed_in = rms_normed(middle)
        piece = lax.all_gather(mixed_in, "tp", axis=0, tiled=True)
        gate = jnp.dot(piece, gate_weight, preferred_element_type=jnp.float32)
        upward = jnp.dot(piece, up_weight, preferred_element_type=jnp.float32)
        hidden = (jax.nn.silu(gate) * upward).astype(jnp.bfloat16)
        lowered = lax.psum_scatter(
            jnp.dot(hidden, down_weight, preferred_element_type=jnp.float32).astype(jnp.bfloat16),
            "tp",
            scatter_dimension=0,
            tiled=True,
        ).astype(jnp.float32)
        results.append((middle + lowered).astype(jnp.bfloat16))
    return jnp.stack(results)

MESH = pl.DeviceIdType.MESH
CHUNK = 4
KEY_BLOCK = 2048
HEAD_ROWS = 16


def greet(axes):
    barrier = pltpu.get_barrier_semaphore()
    total = 0
    for axis, count in axes:
        me = lax.axis_index(axis)
        for hop in range(1, count):
            peer = lax.rem(me + hop, count)
            pl.semaphore_signal(barrier, inc=1, device_id={axis: peer}, device_id_type=MESH)
        total += count - 1
    pl.semaphore_wait(barrier, total)


def start_exchange(axis, count, source, target, send_sem, recv_sem):
    me = lax.axis_index(axis)
    copies = []
    for hop in range(1, count):
        peer = lax.rem(me + hop, count)
        copy = pltpu.make_async_remote_copy(
            src_ref=source(peer),
            dst_ref=target(me),
            send_sem=send_sem.at[hop - 1],
            recv_sem=recv_sem.at[hop - 1],
            device_id={axis: peer},
            device_id_type=MESH,
        )
        copy.start()
        copies.append(copy)
    return copies


def wait_all(copies):
    for copy in copies:
        copy.wait()


def route_kernel(
    req_count, tp_count, pick_ref, x_ref, o_ref, first, second, staged, sends, recvs
):
    req_me = lax.axis_index("req")
    tp_me = lax.axis_index("tp")
    piece = x_ref.shape[1] // tp_count
    greet((("tp", tp_count), ("req", req_count)))

    def columns(peer):
        return x_ref.at[:, pl.ds(pl.multiple_of(peer * piece, piece), piece)]

    copies = start_exchange(
        "tp", tp_count, columns, lambda me: first.at[me], sends.at[0], recvs.at[0]
    )
    first[tp_me] = x_ref[:, pl.ds(pl.multiple_of(tp_me * piece, piece), piece)]
    wait_all(copies)
    group = pl.ds(req_me * tp_count, tp_count)
    copies = start_exchange(
        "req", req_count, lambda peer: first, lambda me: second.at[group], sends.at[1], recvs.at[1]
    )
    second[group] = first[...]
    wait_all(copies)
    for target in range(tp_count):
        staged[target] = second[pick_ref[target]]
    copies = start_exchange(
        "tp",
        tp_count,
        lambda peer: staged.at[peer],
        lambda me: o_ref.at[me],
        sends.at[2],
        recvs.at[2],
    )
    o_ref[tp_me] = staged[tp_me]
    wait_all(copies)


def route(x, pick, req_count, tp_count):
    rows, width = x.shape
    piece = width // tp_count
    most = max(req_count, tp_count)
    return pl.pallas_call(
        functools.partial(route_kernel, req_count, tp_count),
        out_shape=jax.ShapeDtypeStruct((tp_count, rows, piece), x.dtype),
        in_specs=[
            pl.BlockSpec(memory_space=pltpu.SMEM),
            pl.BlockSpec(memory_space=pltpu.VMEM),
        ],
        out_specs=pl.BlockSpec(memory_space=pltpu.VMEM),
        scratch_shapes=[
            pltpu.VMEM((tp_count, rows, piece), x.dtype),
            pltpu.VMEM((req_count * tp_count, rows, piece), x.dtype),
            pltpu.VMEM((tp_count, rows, piece), x.dtype),
            pltpu.SemaphoreType.DMA((3, most)),
            pltpu.SemaphoreType.DMA((3, most)),
        ],
        compiler_params=pltpu.CompilerParams(
            collective_id=0, has_side_effects=True, vmem_limit_bytes=32 * 1024 * 1024
        ),
        name="route",
    )(pick, x)


def attention_kernel(
    pairs,
    order_ref,
    begin_ref,
    count_ref,
    limit_ref,
    beam_ref,
    block_ref,
    total_ref,
    q_ref,
    kn_ref,
    vn_ref,
    seen_ref,
    k_ref,
    v_ref,
    o_ref,
    qs,
    top_s,
    sum_s,
    acc_s,
):
    item = pl.program_id(0)
    head_dim = o_ref.shape[-1]
    width = q_ref.shape[-1]
    scale = head_dim ** (-0.5)
    contract = (((1,), (1,)), ((), ()))
    key_block = k_ref.shape[0]

    @pl.when(item == 0)
    def _():
        for place in range(pairs):
            qs[place] = q_ref[order_ref[place]]
        qs[pairs:] = jnp.zeros((CHUNK,) + qs.shape[1:], qs.dtype)
        rows = pairs * HEAD_ROWS
        scores = scale * lax.dot_general(
            qs[:pairs].reshape(rows, width),
            kn_ref[...],
            contract,
            preferred_element_type=jnp.float32,
        )
        seen = seen_ref[...] > 0.5
        scores = jnp.where(seen, scores, masked_score)
        top = jnp.max(scores, axis=1, keepdims=True)
        weights = jnp.where(seen, jnp.exp(scores - top), 0.0)
        total = jnp.sum(weights, axis=1, keepdims=True)
        mixed = jnp.dot(
            weights.astype(jnp.bfloat16), vn_ref[...], preferred_element_type=jnp.float32
        )
        top_s[:pairs] = jnp.broadcast_to(top, (rows, 128)).reshape(pairs, HEAD_ROWS, 128)
        sum_s[:pairs] = jnp.broadcast_to(total, (rows, 128)).reshape(pairs, HEAD_ROWS, 128)
        acc_s[:pairs] = mixed.reshape(pairs, HEAD_ROWS, width)
        top_s[pairs:] = jnp.zeros((CHUNK, HEAD_ROWS, 128), jnp.float32)
        sum_s[pairs:] = jnp.zeros((CHUNK, HEAD_ROWS, 128), jnp.float32)
        acc_s[pairs:] = jnp.zeros((CHUNK, HEAD_ROWS, width), jnp.float32)

    @pl.when(item < total_ref[0])
    def _():
        beam = beam_ref[item]
        begin = begin_ref[beam]
        end = begin + count_ref[beam]
        left = limit_ref[beam] - block_ref[item] * key_block
        rows = CHUNK * HEAD_ROWS

        def one_chunk(index, carry):
            base = begin + index * CHUNK
            span = pl.ds(base, CHUNK)
            scores = scale * lax.dot_general(
                qs[span].reshape(rows, width),
                k_ref[...],
                contract,
                preferred_element_type=jnp.float32,
            )
            place = lax.broadcasted_iota(jnp.int32, (rows, key_block), 1)
            row = lax.broadcasted_iota(jnp.int32, (rows, 1), 0)
            live = place < jnp.where(row < (end - base) * HEAD_ROWS, left, 0)
            scores = jnp.where(live, scores, masked_score)
            old = top_s[span].reshape(rows, 128)[:, :1]
            top = jnp.maximum(old, jnp.max(scores, axis=1, keepdims=True))
            weights = jnp.where(live, jnp.exp(scores - top), 0.0)
            fade = jnp.exp(old - top)
            total = sum_s[span].reshape(rows, 128)[:, :1] * fade
            total = total + jnp.sum(weights, axis=1, keepdims=True)
            mixed = acc_s[span].reshape(rows, width) * fade + jnp.dot(
                weights.astype(jnp.bfloat16), v_ref[...], preferred_element_type=jnp.float32
            )
            top_s[span] = jnp.broadcast_to(top, (rows, 128)).reshape(CHUNK, HEAD_ROWS, 128)
            sum_s[span] = jnp.broadcast_to(total, (rows, 128)).reshape(CHUNK, HEAD_ROWS, 128)
            acc_s[span] = mixed.reshape(CHUNK, HEAD_ROWS, width)
            return carry

        lax.fori_loop(0, lax.div(end - begin + CHUNK - 1, CHUNK), one_chunk, 0)

    @pl.when(item == pl.num_programs(0) - 1)
    def _():
        row = lax.broadcasted_iota(jnp.int32, (HEAD_ROWS, head_dim), 0)
        for place in range(pairs):
            mixed = acc_s[place] / sum_s[place][:, :1]
            own = jnp.where(
                row < Q_HEADS // KV_HEADS, mixed[:, :head_dim], mixed[:, head_dim:]
            )
            o_ref[order_ref[place]] = own.astype(o_ref.dtype)


def request_plan(parents, lengths, context, key_block):
    steps_count, beams = parents.shape
    beam_range = jnp.arange(beams, dtype=jnp.int32)
    pairs = steps_count * beams

    def follow(before, step):
        hit = parents[step][:, None] == beam_range[None, :]
        return jnp.sum(jnp.where(hit, before[None, :], 0), axis=1)

    root = beam_range
    roots = []
    live_from = []
    seen = []
    for step in range(steps_count):
        root = follow(root, step)
        roots.append(root)
        live_from = [follow(before, step) for before in live_from] + [beam_range]
        blocks = [
            (before[:, None] == beam_range[None, :]).astype(jnp.float32) for before in live_from
        ]
        blocks += [jnp.zeros((beams, beams), jnp.float32)] * (steps_count - step - 1)
        seen.append(jnp.concatenate(blocks, axis=1))
    seen = jnp.concatenate(seen, axis=0)
    flat = jnp.concatenate(roots)
    index = jnp.arange(pairs, dtype=jnp.int32)
    before = (flat[None, :] < flat[:, None]) | (
        (flat[None, :] == flat[:, None]) & (index[None, :] < index[:, None])
    )
    rank = jnp.sum(before.astype(jnp.int32), axis=1)
    hit = rank[None, :] == index[:, None]
    order = jnp.sum(jnp.where(hit, index[None, :], 0), axis=1)
    seen = jnp.sum(jnp.where(hit[:, :, None], seen[None], 0.0), axis=1)
    seen = jnp.repeat(seen, HEAD_ROWS, axis=0)
    begin = jnp.sum((flat[None, :] < beam_range[:, None]).astype(jnp.int32), axis=1)
    count = jnp.sum((flat[None, :] == beam_range[:, None]).astype(jnp.int32), axis=1)
    per_beam = context // key_block
    items = jnp.arange(beams * per_beam, dtype=jnp.int32)
    first = jnp.arange(per_beam, dtype=jnp.int32) * key_block
    valid = ((count > 0)[:, None] & (first[None, :] < lengths[:, None])).reshape(-1)
    total = jnp.sum(valid.astype(jnp.int32))
    ahead = jnp.sum(
        (valid[None, :] & (items[None, :] < items[:, None])).astype(jnp.int32), axis=1
    )
    wanted = jnp.minimum(items, total - 1)
    chosen = valid[None, :] & (ahead[None, :] == wanted[:, None])
    chosen = jnp.sum(jnp.where(chosen, items[None, :], 0), axis=1)
    return (
        order,
        begin,
        count,
        lengths,
        chosen // per_beam,
        chosen % per_beam,
        total.reshape(1),
        seen,
    )


def beam_attention(queries, new_keys, new_values, cache_keys, cache_values, plan, key_block):
    pairs, heads, head_dim = queries.shape
    beams, context, width = cache_keys.shape
    group = heads // KV_HEADS
    scalars, seen = plan[:-1], plan[-1]
    zero = jnp.zeros((pairs, group, head_dim), queries.dtype)
    spread = jnp.concatenate(
        [
            jnp.concatenate([queries[:, :group], zero], axis=2),
            jnp.concatenate([zero, queries[:, group:]], axis=2),
            jnp.zeros((pairs, HEAD_ROWS - heads, width), queries.dtype),
        ],
        axis=1,
    )

    def whole(shape):
        return pl.BlockSpec(shape, lambda i, *refs: (0,) * len(shape))

    def cached(i, order, begin, count, limit, beam, block, total):
        return (beam[i], block[i], 0)

    items = scalars[4].shape[0]
    return pl.pallas_call(
        functools.partial(attention_kernel, pairs),
        out_shape=jax.ShapeDtypeStruct((pairs, HEAD_ROWS, head_dim), jnp.bfloat16),
        grid_spec=pltpu.PrefetchScalarGridSpec(
            num_scalar_prefetch=7,
            grid=(items,),
            in_specs=[
                whole(spread.shape),
                whole(new_keys.shape),
                whole(new_values.shape),
                whole(seen.shape),
                pl.BlockSpec((None, key_block, width), cached),
                pl.BlockSpec((None, key_block, width), cached),
            ],
            out_specs=whole((pairs, HEAD_ROWS, head_dim)),
            scratch_shapes=[
                pltpu.VMEM((pairs + CHUNK, HEAD_ROWS, width), jnp.bfloat16),
                pltpu.VMEM((pairs + CHUNK, HEAD_ROWS, 128), jnp.float32),
                pltpu.VMEM((pairs + CHUNK, HEAD_ROWS, 128), jnp.float32),
                pltpu.VMEM((pairs + CHUNK, HEAD_ROWS, width), jnp.float32),
            ],
        ),
        compiler_params=pltpu.CompilerParams(vmem_limit_bytes=32 * 1024 * 1024),
        name="beam_attention",
    )(*scalars, spread, new_keys, new_values, seen, cache_keys, cache_values)[:, :heads]


def layer_kernel(
    req_count,
    tp_count,
    pick_ref,
    att_ref,
    x_ref,
    ow_ref,
    gw_hbm,
    uw_hbm,
    dw_hbm,
    o_ref,
    first,
    second,
    part,
    landed_a,
    mixed,
    landed_b,
    gw,
    uw,
    dw,
    picked,
    sends,
    recvs,
    load_sems,
):
    req_me = lax.axis_index("req")
    tp_me = lax.axis_index("tp")
    rows, width = x_ref.shape
    loads = [
        pltpu.make_async_copy(far, near, load_sems.at[index])
        for index, (far, near) in enumerate(((gw_hbm, gw), (uw_hbm, uw), (dw_hbm, dw)))
    ]
    for load in loads:
        load.start()
    greet((("tp", tp_count), ("req", req_count)))
    copies = start_exchange(
        "tp",
        tp_count,
        lambda peer: att_ref.at[peer],
        lambda me: first.at[me],
        sends.at[0],
        recvs.at[0],
    )
    first[tp_me] = att_ref[tp_me]
    wait_all(copies)
    group = pl.ds(req_me * tp_count, tp_count)
    copies = start_exchange(
        "req", req_count, lambda peer: first, lambda me: second.at[group], sends.at[1], recvs.at[1]
    )
    second[group] = first[...]
    wait_all(copies)
    for slot in range(tp_count):
        picked[slot] = second[pick_ref[slot]]
    part[...] = (
        jnp.dot(
            picked[...].reshape(tp_count * rows, picked.shape[2]),
            ow_ref[...],
            preferred_element_type=jnp.float32,
        )
        .astype(jnp.bfloat16)
        .reshape(part.shape)
    )
    copies = start_exchange(
        "tp",
        tp_count,
        lambda peer: part.at[peer],
        lambda me: landed_a.at[me],
        sends.at[2],
        recvs.at[2],
    )
    landed_a[tp_me] = part[tp_me]
    wait_all(copies)
    middle = x_ref[...].astype(jnp.float32)
    for source in range(tp_count):
        middle = middle + landed_a[source].astype(jnp.float32)
    factor = lax.rsqrt(jnp.mean(middle * middle, axis=-1, keepdims=True) + norm_eps)
    mixed[tp_me] = (middle * factor).astype(jnp.bfloat16)
    copies = start_exchange(
        "tp",
        tp_count,
        lambda peer: mixed.at[tp_me],
        lambda me: mixed.at[me],
        sends.at[3],
        recvs.at[3],
    )
    wait_all(copies)
    for load in loads:
        load.wait()
    half = tp_count // 2

    for turn in range(2):
        span = pl.ds(turn * half, half)
        block = mixed[span].reshape(half * rows, width)
        gate = jnp.dot(block, gw[...], preferred_element_type=jnp.float32)
        upward = jnp.dot(block, uw[...], preferred_element_type=jnp.float32)
        hidden = (gate * jax.nn.sigmoid(gate) * upward).astype(jnp.bfloat16)
        part2 = jnp.dot(hidden, dw[...], preferred_element_type=jnp.float32)
        part[span] = part2.astype(jnp.bfloat16).reshape(half, rows, width)
    copies = start_exchange(
        "tp",
        tp_count,
        lambda peer: part.at[peer],
        lambda me: landed_b.at[me],
        sends.at[4],
        recvs.at[4],
    )
    landed_b[tp_me] = part[tp_me]
    wait_all(copies)
    lowered = landed_b[0].astype(jnp.float32)
    for source in range(1, tp_count):
        lowered = lowered + landed_b[source].astype(jnp.float32)
    o_ref[...] = (middle + lowered).astype(o_ref.dtype)


def layer(attention, pick, x, out_weight, gate_weight, up_weight, down_weight, req_count, tp_count):
    rows, width = x.shape
    piece = attention.shape[2]
    most = max(req_count, tp_count)
    vmem = pl.BlockSpec(memory_space=pltpu.VMEM)
    far = pl.BlockSpec(memory_space=pl.ANY)
    blocks = (tp_count, rows, width)
    return pl.pallas_call(
        functools.partial(layer_kernel, req_count, tp_count),
        out_shape=jax.ShapeDtypeStruct((rows, width), jnp.bfloat16),
        in_specs=[pl.BlockSpec(memory_space=pltpu.SMEM), vmem, vmem, vmem, far, far, far],
        out_specs=vmem,
        scratch_shapes=[
            pltpu.VMEM((tp_count, rows, piece), jnp.bfloat16),
            pltpu.VMEM((req_count * tp_count, rows, piece), jnp.bfloat16),
            pltpu.VMEM(blocks, jnp.bfloat16),
            pltpu.VMEM(blocks, jnp.bfloat16),
            pltpu.VMEM(blocks, jnp.bfloat16),
            pltpu.VMEM(blocks, jnp.bfloat16),
            pltpu.VMEM(gate_weight.shape, jnp.bfloat16),
            pltpu.VMEM(up_weight.shape, jnp.bfloat16),
            pltpu.VMEM(down_weight.shape, jnp.bfloat16),
            pltpu.VMEM((tp_count, rows, piece), jnp.bfloat16),
            pltpu.SemaphoreType.DMA((5, most)),
            pltpu.SemaphoreType.DMA((5, most)),
            pltpu.SemaphoreType.DMA((3,)),
        ],
        compiler_params=pltpu.CompilerParams(
            collective_id=1, has_side_effects=True, vmem_limit_bytes=48 * 1024 * 1024
        ),
        name="layer",
    )(pick, attention, x, out_weight, gate_weight, up_weight, down_weight)


def per_device_whole(
    step_inputs,
    qkv_weight,
    qkv_bias,
    out_weight,
    gate_weight,
    up_weight,
    down_weight,
    cache_keys,
    cache_values,
    lengths,
    parents,
    slot_request,
):
    steps_count, beams, width = step_inputs.shape
    requests = slot_request.shape[0]
    req_count = lax.axis_size("req")
    tp_count = lax.axis_size("tp")
    context, kv_width = cache_keys.shape[1:]
    head_dim = kv_width // KV_HEADS
    attn_width = Q_HEADS * head_dim
    req_index = lax.axis_index("req")
    flat_index = req_index * tp_count + lax.axis_index("tp")
    rows = steps_count * beams
    key_block = min(KEY_BLOCK, context)
    request_range = jnp.arange(requests, dtype=jnp.int32)
    inverse = jnp.sum(
        jnp.where(slot_request[None, :] == request_range[:, None], request_range[None, :], 0),
        axis=1,
    )
    group_base = req_index * tp_count
    pick_slots = lax.dynamic_slice_in_dim(inverse, group_base, tp_count)
    pick_requests = lax.dynamic_slice_in_dim(slot_request, group_base, tp_count)

    mine = slot_request[flat_index]
    my_parents = lax.dynamic_index_in_dim(parents, mine, 1, keepdims=False)
    my_lengths = lax.dynamic_index_in_dim(lengths, mine, 0, keepdims=False)
    beam_range = jnp.arange(beams, dtype=jnp.int32)
    positions = []
    root_length = my_lengths
    for step in range(steps_count):
        hit = my_parents[step][:, None] == beam_range[None, :]
        root_length = jnp.sum(jnp.where(hit, root_length[None, :], 0), axis=1)
        positions.append(root_length + step)
    positions = jnp.concatenate(positions)

    inputs = step_inputs.reshape(rows, width)
    qkv = (
        jnp.dot(rms_normed(inputs), qkv_weight, preferred_element_type=jnp.float32) + qkv_bias
    ).astype(jnp.bfloat16)
    turned_width = attn_width + kv_width
    turned = rotate(qkv[:, :turned_width].reshape(rows, -1, head_dim), positions)
    packed = jnp.concatenate([turned.reshape(rows, turned_width), qkv[:, turned_width:]], axis=1)
    routed = route(packed, pick_slots, req_count, tp_count)
    routed = routed.transpose(1, 0, 2).reshape(rows, -1)

    own_parents = lax.dynamic_index_in_dim(parents, flat_index, 1, keepdims=False)
    own_lengths = lax.dynamic_index_in_dim(lengths, flat_index, 0, keepdims=False)
    plan = request_plan(own_parents, own_lengths, context, key_block)
    attention = beam_attention(
        routed[:, :attn_width].reshape(rows, Q_HEADS, head_dim),
        routed[:, attn_width:turned_width],
        routed[:, turned_width:],
        cache_keys,
        cache_values,
        plan,
        key_block,
    )
    pieces = attention.reshape(rows, tp_count, attn_width // tp_count).transpose(1, 0, 2)
    result = layer(
        pieces,
        pick_requests,
        inputs,
        out_weight,
        gate_weight,
        up_weight,
        down_weight,
        req_count,
        tp_count,
    )
    return result.reshape(steps_count, beams, width)


def per_device(*arrays):
    step_inputs, qkv_weight, cache_keys, parents = arrays[0], arrays[1], arrays[7], arrays[10]
    beams = parents.shape[2]
    tp_count = lax.axis_size("tp")
    whole = (
        step_inputs.shape[1] == beams
        and cache_keys.shape[0] == beams
        and tp_count % 2 == 0
        and qkv_weight.shape[1] % (128 * tp_count) == 0
        and cache_keys.shape[1] % min(KEY_BLOCK, cache_keys.shape[1]) == 0
    )
    return (per_device_whole if whole else per_device_split)(*arrays)


def solution(mesh):
    in_specs = (
        P(None, ("req", "tp"), None),
        P(),
        P(),
        P("tp", None),
        P(None, "tp"),
        P(None, "tp"),
        P("tp", None),
        P(("req", "tp"), None, None),
        P(("req", "tp"), None, None),
        P(),
        P(),
        P(),
    )
    out_specs = P(None, ("req", "tp"), None)
    return jax.shard_map(
        per_device, mesh=mesh, in_specs=in_specs, out_specs=out_specs, check_vma=False
    )
```

```python
import functools

import jax
import jax.numpy as jnp
from jax import lax
from jax.experimental import pallas as pl
from jax.experimental.pallas import tpu as pltpu
from jax.sharding import PartitionSpec as P

Q_HEADS = 12
KV_HEADS = 2


theta_base = 1000000.0
norm_eps = 1e-06
masked_score = -1e30


def rms_normed(values):
    values = values.astype(jnp.float32)
    factor = lax.rsqrt(jnp.mean(values * values, axis=-1, keepdims=True) + norm_eps)
    return (values * factor).astype(jnp.bfloat16)


def rotate(vectors, positions):
    half = vectors.shape[-1] // 2
    freqs = theta_base ** (-jnp.arange(half, dtype=jnp.float32) * 2.0 / vectors.shape[-1])
    angles = positions.astype(jnp.float32)[:, None] * freqs[None, :]
    cosine = jnp.cos(angles)[:, None, :]
    sine = jnp.sin(angles)[:, None, :]
    values = vectors.astype(jnp.float32)
    first = values[..., :half]
    second = values[..., half:]
    return jnp.concatenate(
        [first * cosine - second * sine, second * cosine + first * sine], axis=-1
    ).astype(jnp.bfloat16)


def owner_rows(flat, owned_count, beams, inverse):
    owned_global = flat * owned_count + jnp.arange(owned_count, dtype=jnp.int32)
    owned_request = owned_global // beams
    owned_beam = owned_global % beams
    beam_range = jnp.arange(beams, dtype=jnp.int32)
    query_rows = (inverse[owned_request][:, None] * beams + beam_range[None, :]).reshape(-1)
    return (owned_request, owned_beam, query_rows)


def owned_attention(
    every_query, keys, values, owned_request, owned_beam, query_rows, root_all, lengths
):
    owned_rows, context, kv_width = keys.shape
    beams = root_all.shape[1]
    head_dim = kv_width // KV_HEADS
    group = Q_HEADS // KV_HEADS
    grouped = jnp.take(every_query, query_rows, axis=0).reshape(
        owned_rows, beams, KV_HEADS, group, head_dim
    )
    keys = keys.reshape(owned_rows, context, KV_HEADS, head_dim)
    values = values.reshape(owned_rows, context, KV_HEADS, head_dim)
    scores = jnp.einsum(
        "jbkgd,jpkd->jbkgp", grouped, keys, preferred_element_type=jnp.float32
    ) * head_dim ** (-0.5)
    limits = lengths[owned_request, owned_beam]
    live = (jnp.arange(context, dtype=jnp.int32)[None, :] < limits[:, None])[:, None, None, None, :]
    scores = jnp.where(live, scores, masked_score)
    peak = jnp.max(scores, axis=-1)
    weights = jnp.where(live, jnp.exp(scores - peak[..., None]), 0.0)
    total = jnp.sum(weights, axis=-1)
    output = jnp.einsum(
        "jbkgp,jpkd->jbkgd",
        weights.astype(jnp.bfloat16),
        values,
        preferred_element_type=jnp.float32,
    )
    chosen = (root_all[owned_request] == owned_beam[:, None])[:, :, None, None]
    peak = jnp.where(chosen, peak, 0.0).reshape(owned_rows * beams, KV_HEADS, group)
    total = jnp.where(chosen, total, 0.0).reshape(owned_rows * beams, KV_HEADS, group)
    output = jnp.where(chosen[..., None], output, 0.0).reshape(
        owned_rows * beams, KV_HEADS, group, head_dim
    )
    return (peak, total, output)


def spread_rows(pieces, target_rows, row_count):
    return tuple(
        (
            jnp.zeros((row_count,) + piece.shape[1:], jnp.float32).at[target_rows].add(piece)
            for piece in pieces
        )
    )


def per_device_split(
    step_inputs,
    qkv_weight,
    qkv_bias,
    out_weight,
    gate_weight,
    up_weight,
    down_weight,
    cache_keys,
    cache_values,
    lengths,
    parents,
    slot_request,
):
    steps_count, rows_dev, width = step_inputs.shape
    beams = parents.shape[2]
    requests = slot_request.shape[0]
    req_count = lax.axis_size("req")
    tp_count = lax.axis_size("tp")
    group_requests = requests // req_count
    group_rows = group_requests * beams
    total_rows = requests * beams
    owned_count = cache_keys.shape[0]
    kv_width = cache_keys.shape[2]
    head_dim = kv_width // KV_HEADS
    group = Q_HEADS // KV_HEADS
    attn_width = Q_HEADS * head_dim
    req_index = lax.axis_index("req")
    tp_index = lax.axis_index("tp")
    flat_index = req_index * tp_count + tp_index
    my_requests = lax.dynamic_slice_in_dim(slot_request, req_index * group_requests, group_requests)
    inverse = (
        jnp.zeros((requests,), jnp.int32)
        .at[slot_request]
        .set(jnp.arange(requests, dtype=jnp.int32))
    )
    owned_request, owned_beam, query_rows = owner_rows(flat_index, owned_count, beams, inverse)
    beam_range = jnp.arange(beams, dtype=jnp.int32)
    root_all = jnp.broadcast_to(beam_range[None, :], (requests, beams))
    gen_keys = jnp.zeros((steps_count, group_rows, kv_width), jnp.bfloat16)
    gen_values = jnp.zeros((steps_count, group_rows, kv_width), jnp.bfloat16)
    base_rows = (jnp.arange(group_requests, dtype=jnp.int32) * beams)[:, None]
    column_width = out_weight.shape[0]
    results = []
    for step in range(steps_count):
        root_all = jnp.take_along_axis(root_all, parents[step], axis=1)
        reorder = (base_rows + parents[step][my_requests]).reshape(-1)
        gen_keys = jnp.take(gen_keys, reorder, axis=1)
        gen_values = jnp.take(gen_values, reorder, axis=1)
        inputs = step_inputs[step]
        normed = rms_normed(inputs)
        qkv = (
            jnp.dot(
                lax.all_gather(normed, "tp", axis=0, tiled=True),
                qkv_weight,
                preferred_element_type=jnp.float32,
            )
            + qkv_bias
        ).astype(jnp.bfloat16)
        my_roots = root_all[my_requests]
        positions = (jnp.take_along_axis(lengths[my_requests], my_roots, axis=1) + step).reshape(-1)
        queries = rotate(qkv[:, :attn_width].reshape(group_rows, Q_HEADS, head_dim), positions)
        new_keys = rotate(
            qkv[:, attn_width : attn_width + kv_width].reshape(group_rows, KV_HEADS, head_dim),
            positions,
        )
        gen_keys = gen_keys.at[step].set(new_keys.reshape(group_rows, kv_width))
        gen_values = gen_values.at[step].set(qkv[:, attn_width + kv_width :])
        every_query = lax.all_gather(
            queries.reshape(group_rows, attn_width), "req", axis=0, tiled=True
        )
        part_peak, part_total, part_output = owned_attention(
            every_query,
            cache_keys,
            cache_values,
            owned_request,
            owned_beam,
            query_rows,
            root_all,
            lengths,
        )
        all_peak, all_total, all_output = spread_rows(
            (part_peak, part_total, part_output), query_rows, total_rows
        )
        sum_peak, sum_total, sum_output = lax.psum((all_peak, all_total, all_output), ("req", "tp"))
        peak = lax.dynamic_slice_in_dim(sum_peak, req_index * group_rows, group_rows, 0)
        total = lax.dynamic_slice_in_dim(sum_total, req_index * group_rows, group_rows, 0)
        output = lax.dynamic_slice_in_dim(sum_output, req_index * group_rows, group_rows, 0)
        grouped = queries.reshape(group_rows, KV_HEADS, group, head_dim)
        past_keys = gen_keys[: step + 1].reshape(step + 1, group_rows, KV_HEADS, head_dim)
        past_values = gen_values[: step + 1].reshape(step + 1, group_rows, KV_HEADS, head_dim)
        recent_scores = jnp.einsum(
            "bkgd,sbkd->bkgs", grouped, past_keys, preferred_element_type=jnp.float32
        ) * head_dim ** (-0.5)
        top = jnp.maximum(peak, jnp.max(recent_scores, axis=-1))
        factor = jnp.exp(peak - top)
        recent_weights = jnp.exp(recent_scores - top[..., None])
        denominator = total * factor + jnp.sum(recent_weights, axis=-1)
        numerator = output * factor[..., None] + jnp.einsum(
            "bkgs,sbkd->bkgd",
            recent_weights.astype(jnp.bfloat16),
            past_values,
            preferred_element_type=jnp.float32,
        )
        attention = (
            (numerator / denominator[..., None])
            .reshape(group_rows, attn_width)
            .astype(jnp.bfloat16)
        )
        columns = lax.dynamic_slice_in_dim(attention, tp_index * column_width, column_width, 1)
        attended = lax.psum_scatter(
            jnp.dot(columns, out_weight, preferred_element_type=jnp.float32).astype(jnp.bfloat16),
            "tp",
            scatter_dimension=0,
            tiled=True,
        ).astype(jnp.float32)
        middle = inputs.astype(jnp.float32) + attended
        mixed_in = rms_normed(middle)
        piece = lax.all_gather(mixed_in, "tp", axis=0, tiled=True)
        gate = jnp.dot(piece, gate_weight, preferred_element_type=jnp.float32)
        upward = jnp.dot(piece, up_weight, preferred_element_type=jnp.float32)
        hidden = (jax.nn.silu(gate) * upward).astype(jnp.bfloat16)
        lowered = lax.psum_scatter(
            jnp.dot(hidden, down_weight, preferred_element_type=jnp.float32).astype(jnp.bfloat16),
            "tp",
            scatter_dimension=0,
            tiled=True,
        ).astype(jnp.float32)
        results.append((middle + lowered).astype(jnp.bfloat16))
    return jnp.stack(results)

MESH = pl.DeviceIdType.MESH
CHUNK = 4
KEY_BLOCK = 2048
HEAD_ROWS = 16


def greet(axes):
    barrier = pltpu.get_barrier_semaphore()
    total = 0
    for axis, count in axes:
        me = lax.axis_index(axis)
        for hop in range(1, count):
            peer = lax.rem(me + hop, count)
            pl.semaphore_signal(barrier, inc=1, device_id={axis: peer}, device_id_type=MESH)
        total += count - 1
    pl.semaphore_wait(barrier, total)


def start_exchange(axis, count, source, target, send_sem, recv_sem):
    me = lax.axis_index(axis)
    copies = []
    for hop in range(1, count):
        peer = lax.rem(me + hop, count)
        copy = pltpu.make_async_remote_copy(
            src_ref=source(peer),
            dst_ref=target(me),
            send_sem=send_sem.at[hop - 1],
            recv_sem=recv_sem.at[hop - 1],
            device_id={axis: peer},
            device_id_type=MESH,
        )
        copy.start()
        copies.append(copy)
    return copies


def wait_all(copies):
    for copy in copies:
        copy.wait()


def route_kernel(
    req_count, tp_count, pick_ref, x_ref, o_ref, first, second, staged, sends, recvs
):
    req_me = lax.axis_index("req")
    tp_me = lax.axis_index("tp")
    piece = x_ref.shape[1] // tp_count
    greet((("tp", tp_count), ("req", req_count)))

    def columns(peer):
        return x_ref.at[:, pl.ds(pl.multiple_of(peer * piece, piece), piece)]

    copies = start_exchange(
        "tp", tp_count, columns, lambda me: first.at[me], sends.at[0], recvs.at[0]
    )
    first[tp_me] = x_ref[:, pl.ds(pl.multiple_of(tp_me * piece, piece), piece)]
    wait_all(copies)
    group = pl.ds(req_me * tp_count, tp_count)
    copies = start_exchange(
        "req", req_count, lambda peer: first, lambda me: second.at[group], sends.at[1], recvs.at[1]
    )
    second[group] = first[...]
    wait_all(copies)
    for target in range(tp_count):
        staged[target] = second[pick_ref[target]]
    copies = start_exchange(
        "tp",
        tp_count,
        lambda peer: staged.at[peer],
        lambda me: o_ref.at[me],
        sends.at[2],
        recvs.at[2],
    )
    o_ref[tp_me] = staged[tp_me]
    wait_all(copies)


def route(x, pick, req_count, tp_count):
    rows, width = x.shape
    piece = width // tp_count
    most = max(req_count, tp_count)
    return pl.pallas_call(
        functools.partial(route_kernel, req_count, tp_count),
        out_shape=jax.ShapeDtypeStruct((tp_count, rows, piece), x.dtype),
        in_specs=[
            pl.BlockSpec(memory_space=pltpu.SMEM),
            pl.BlockSpec(memory_space=pltpu.VMEM),
        ],
        out_specs=pl.BlockSpec(memory_space=pltpu.VMEM),
        scratch_shapes=[
            pltpu.VMEM((tp_count, rows, piece), x.dtype),
            pltpu.VMEM((req_count * tp_count, rows, piece), x.dtype),
            pltpu.VMEM((tp_count, rows, piece), x.dtype),
            pltpu.SemaphoreType.DMA((3, most)),
            pltpu.SemaphoreType.DMA((3, most)),
        ],
        compiler_params=pltpu.CompilerParams(
            collective_id=0, has_side_effects=True, vmem_limit_bytes=32 * 1024 * 1024
        ),
        name="route",
    )(pick, x)


def attention_kernel(
    pairs,
    order_ref,
    begin_ref,
    count_ref,
    limit_ref,
    beam_ref,
    block_ref,
    total_ref,
    q_ref,
    kn_ref,
    vn_ref,
    seen_ref,
    k_ref,
    v_ref,
    o_ref,
    qs,
    top_s,
    sum_s,
    acc_s,
):
    item = pl.program_id(0)
    head_dim = o_ref.shape[-1]
    width = q_ref.shape[-1]
    scale = head_dim ** (-0.5)
    contract = (((1,), (1,)), ((), ()))
    key_block = k_ref.shape[0]

    @pl.when(item == 0)
    def _():
        for place in range(pairs):
            qs[place] = q_ref[order_ref[place]]
        qs[pairs:] = jnp.zeros((CHUNK,) + qs.shape[1:], qs.dtype)
        rows = pairs * HEAD_ROWS
        scores = scale * lax.dot_general(
            qs[:pairs].reshape(rows, width),
            kn_ref[...],
            contract,
            preferred_element_type=jnp.float32,
        )
        seen = seen_ref[...] > 0.5
        scores = jnp.where(seen, scores, masked_score)
        top = jnp.max(scores, axis=1, keepdims=True)
        weights = jnp.where(seen, jnp.exp(scores - top), 0.0)
        total = jnp.sum(weights, axis=1, keepdims=True)
        mixed = jnp.dot(
            weights.astype(jnp.bfloat16), vn_ref[...], preferred_element_type=jnp.float32
        )
        top_s[:pairs] = jnp.broadcast_to(top, (rows, 128)).reshape(pairs, HEAD_ROWS, 128)
        sum_s[:pairs] = jnp.broadcast_to(total, (rows, 128)).reshape(pairs, HEAD_ROWS, 128)
        acc_s[:pairs] = mixed.reshape(pairs, HEAD_ROWS, width)
        top_s[pairs:] = jnp.zeros((CHUNK, HEAD_ROWS, 128), jnp.float32)
        sum_s[pairs:] = jnp.zeros((CHUNK, HEAD_ROWS, 128), jnp.float32)
        acc_s[pairs:] = jnp.zeros((CHUNK, HEAD_ROWS, width), jnp.float32)

    @pl.when(item < total_ref[0])
    def _():
        beam = beam_ref[item]
        begin = begin_ref[beam]
        end = begin + count_ref[beam]
        left = limit_ref[beam] - block_ref[item] * key_block
        rows = CHUNK * HEAD_ROWS

        def one_chunk(index, carry):
            base = begin + index * CHUNK
            span = pl.ds(base, CHUNK)
            scores = scale * lax.dot_general(
                qs[span].reshape(rows, width),
                k_ref[...],
                contract,
                preferred_element_type=jnp.float32,
            )
            place = lax.broadcasted_iota(jnp.int32, (rows, key_block), 1)
            row = lax.broadcasted_iota(jnp.int32, (rows, 1), 0)
            live = place < jnp.where(row < (end - base) * HEAD_ROWS, left, 0)
            scores = jnp.where(live, scores, masked_score)
            old = top_s[span].reshape(rows, 128)[:, :1]
            top = jnp.maximum(old, jnp.max(scores, axis=1, keepdims=True))
            weights = jnp.exp(scores - top)
            fade = jnp.exp(old - top)
            total = sum_s[span].reshape(rows, 128)[:, :1] * fade
            total = total + jnp.sum(weights, axis=1, keepdims=True)
            mixed = acc_s[span].reshape(rows, width) * fade + jnp.dot(
                weights.astype(jnp.bfloat16), v_ref[...], preferred_element_type=jnp.float32
            )
            top_s[span] = jnp.broadcast_to(top, (rows, 128)).reshape(CHUNK, HEAD_ROWS, 128)
            sum_s[span] = jnp.broadcast_to(total, (rows, 128)).reshape(CHUNK, HEAD_ROWS, 128)
            acc_s[span] = mixed.reshape(CHUNK, HEAD_ROWS, width)
            return carry

        lax.fori_loop(0, lax.div(end - begin + CHUNK - 1, CHUNK), one_chunk, 0)

    @pl.when(item == pl.num_programs(0) - 1)
    def _():
        row = lax.broadcasted_iota(jnp.int32, (HEAD_ROWS, head_dim), 0)
        for place in range(pairs):
            mixed = acc_s[place] / sum_s[place][:, :1]
            own = jnp.where(
                row < Q_HEADS // KV_HEADS, mixed[:, :head_dim], mixed[:, head_dim:]
            )
            o_ref[order_ref[place]] = own.astype(o_ref.dtype)


def request_plan(parents, lengths, context, key_block):
    steps_count, beams = parents.shape
    beam_range = jnp.arange(beams, dtype=jnp.int32)
    pairs = steps_count * beams

    def follow(before, step):
        hit = parents[step][:, None] == beam_range[None, :]
        return jnp.sum(jnp.where(hit, before[None, :], 0), axis=1)

    root = beam_range
    roots = []
    live_from = []
    seen = []
    for step in range(steps_count):
        root = follow(root, step)
        roots.append(root)
        live_from = [follow(before, step) for before in live_from] + [beam_range]
        blocks = [
            (before[:, None] == beam_range[None, :]).astype(jnp.float32) for before in live_from
        ]
        blocks += [jnp.zeros((beams, beams), jnp.float32)] * (steps_count - step - 1)
        seen.append(jnp.concatenate(blocks, axis=1))
    seen = jnp.concatenate(seen, axis=0)
    flat = jnp.concatenate(roots)
    index = jnp.arange(pairs, dtype=jnp.int32)
    before = (flat[None, :] < flat[:, None]) | (
        (flat[None, :] == flat[:, None]) & (index[None, :] < index[:, None])
    )
    rank = jnp.sum(before.astype(jnp.int32), axis=1)
    hit = rank[None, :] == index[:, None]
    order = jnp.sum(jnp.where(hit, index[None, :], 0), axis=1)
    seen = jnp.sum(jnp.where(hit[:, :, None], seen[None], 0.0), axis=1)
    seen = jnp.repeat(seen, HEAD_ROWS, axis=0)
    begin = jnp.sum((flat[None, :] < beam_range[:, None]).astype(jnp.int32), axis=1)
    count = jnp.sum((flat[None, :] == beam_range[:, None]).astype(jnp.int32), axis=1)
    per_beam = context // key_block
    items = jnp.arange(beams * per_beam, dtype=jnp.int32)
    first = jnp.arange(per_beam, dtype=jnp.int32) * key_block
    valid = ((count > 0)[:, None] & (first[None, :] < lengths[:, None])).reshape(-1)
    total = jnp.sum(valid.astype(jnp.int32))
    ahead = jnp.sum(
        (valid[None, :] & (items[None, :] < items[:, None])).astype(jnp.int32), axis=1
    )
    wanted = jnp.minimum(items, total - 1)
    chosen = valid[None, :] & (ahead[None, :] == wanted[:, None])
    chosen = jnp.sum(jnp.where(chosen, items[None, :], 0), axis=1)
    return (
        order,
        begin,
        count,
        lengths,
        chosen // per_beam,
        chosen % per_beam,
        total.reshape(1),
        seen,
    )


def beam_attention(queries, new_keys, new_values, cache_keys, cache_values, plan, key_block):
    pairs, heads, head_dim = queries.shape
    beams, context, width = cache_keys.shape
    group = heads // KV_HEADS
    scalars, seen = plan[:-1], plan[-1]
    zero = jnp.zeros((pairs, group, head_dim), queries.dtype)
    spread = jnp.concatenate(
        [
            jnp.concatenate([queries[:, :group], zero], axis=2),
            jnp.concatenate([zero, queries[:, group:]], axis=2),
            jnp.zeros((pairs, HEAD_ROWS - heads, width), queries.dtype),
        ],
        axis=1,
    )

    def whole(shape):
        return pl.BlockSpec(shape, lambda i, *refs: (0,) * len(shape))

    def cached(i, order, begin, count, limit, beam, block, total):
        return (beam[i], block[i], 0)

    items = scalars[4].shape[0]
    return pl.pallas_call(
        functools.partial(attention_kernel, pairs),
        out_shape=jax.ShapeDtypeStruct((pairs, HEAD_ROWS, head_dim), jnp.bfloat16),
        grid_spec=pltpu.PrefetchScalarGridSpec(
            num_scalar_prefetch=7,
            grid=(items,),
            in_specs=[
                whole(spread.shape),
                whole(new_keys.shape),
                whole(new_values.shape),
                whole(seen.shape),
                pl.BlockSpec((None, key_block, width), cached),
                pl.BlockSpec((None, key_block, width), cached),
            ],
            out_specs=whole((pairs, HEAD_ROWS, head_dim)),
            scratch_shapes=[
                pltpu.VMEM((pairs + CHUNK, HEAD_ROWS, width), jnp.bfloat16),
                pltpu.VMEM((pairs + CHUNK, HEAD_ROWS, 128), jnp.float32),
                pltpu.VMEM((pairs + CHUNK, HEAD_ROWS, 128), jnp.float32),
                pltpu.VMEM((pairs + CHUNK, HEAD_ROWS, width), jnp.float32),
            ],
        ),
        compiler_params=pltpu.CompilerParams(vmem_limit_bytes=56 * 1024 * 1024),
        name="beam_attention",
    )(*scalars, spread, new_keys, new_values, seen, cache_keys, cache_values)[:, :heads]


def start_send(source, target, send_sem, recv_sem, peer):
    copy = pltpu.make_async_remote_copy(
        src_ref=source,
        dst_ref=target,
        send_sem=send_sem,
        recv_sem=recv_sem,
        device_id={"tp": peer},
        device_id_type=MESH,
    )
    copy.start()
    return copy


def layer_kernel(
    req_count,
    tp_count,
    pick_ref,
    att_ref,
    x_ref,
    ow_hbm,
    gw_hbm,
    uw_hbm,
    dw_hbm,
    o_ref,
    first,
    second,
    part_a,
    part_b,
    pair_a,
    pair_b,
    joined_a,
    joined_b,
    landed_a,
    landed_b,
    mixed,
    ow,
    gw,
    uw,
    dw,
    sends,
    recvs,
    load_sems,
):
    req_me = lax.axis_index("req")
    tp_me = lax.axis_index("tp")
    chips = tp_count // 2
    chip = tp_me // 2
    core = lax.rem(tp_me, 2)
    other = 1 - core
    partner = chip * 2 + other
    rows, width = x_ref.shape
    weights = ((ow_hbm, ow), (gw_hbm, gw), (uw_hbm, uw), (dw_hbm, dw))
    loads = [
        pltpu.make_async_copy(far, near, load_sems.at[index])
        for index, (far, near) in enumerate(weights)
    ]
    for load in loads:
        load.start()
    greet((("tp", tp_count), ("req", req_count)))
    copies = start_exchange(
        "tp",
        tp_count,
        lambda peer: att_ref.at[peer],
        lambda me: first.at[me],
        sends.at[0],
        recvs.at[0],
    )
    first[tp_me] = att_ref[tp_me]
    wait_all(copies)
    group = pl.ds(req_me * tp_count, tp_count)
    copies = start_exchange(
        "req", req_count, lambda peer: first, lambda me: second.at[group], sends.at[1], recvs.at[1]
    )
    second[group] = first[...]
    wait_all(copies)
    loads[0].wait()
    behind = [lax.rem(chip - hop + chips, chips) for hop in range(chips)]
    ahead = [lax.rem(chip + hop, chips) for hop in range(chips)]
    far_first = list(range(1, chips)) + [0]

    pairs = {}
    for hop in far_first:
        picked = jnp.concatenate(
            [second[pick_ref[behind[hop] * 2 + side]] for side in range(2)], axis=0
        )
        product = jnp.dot(picked, ow[...], preferred_element_type=jnp.float32)
        part_a[hop] = product.astype(jnp.bfloat16).reshape(2, rows, width)
        pairs[hop] = start_send(
            part_a.at[hop, other], pair_a.at[hop], sends.at[2, hop], recvs.at[2, hop], partner
        )
    outs = []
    for hop in far_first:
        pairs[hop].wait()
        both = part_a[hop, core].astype(jnp.float32) + pair_a[hop].astype(jnp.float32)
        if hop:
            joined_a[hop] = both.astype(jnp.bfloat16)
            outs.append(
                start_send(
                    joined_a.at[hop],
                    landed_a.at[hop],
                    sends.at[3, hop],
                    recvs.at[3, hop],
                    behind[hop] * 2 + core,
                )
            )
    wait_all(outs)
    middle = x_ref[...].astype(jnp.float32) + both
    for hop in range(1, chips):
        middle = middle + landed_a[hop].astype(jnp.float32)
    factor = lax.rsqrt(jnp.mean(middle * middle, axis=-1, keepdims=True) + norm_eps)
    mixed[0, core] = (middle * factor).astype(jnp.bfloat16)
    direct = {}
    for hop in range(1, chips):
        direct[hop] = start_send(
            mixed.at[0, core],
            mixed.at[hop, core],
            sends.at[4, hop],
            recvs.at[4, hop],
            ahead[hop] * 2 + core,
        )
    passed = [
        start_send(
            mixed.at[0, core], mixed.at[0, core], sends.at[5, 0], recvs.at[5, 0], partner
        )
    ]

    def take(hop):
        direct[hop].wait()
        passed.append(
            start_send(
                mixed.at[hop, core],
                mixed.at[hop, core],
                sends.at[5, hop],
                recvs.at[5, hop],
                partner,
            )
        )

    half = chips // 2
    for hop in range(1, half):
        take(hop)
    for load in loads[1:]:
        load.wait()
    contract = (((1,), (1,)), ((), ()))
    pairs = {}

    def feed(start):
        block = mixed[start : start + half].reshape(half * 2 * rows, width)
        gate = lax.dot_general(block, gw[...], contract, preferred_element_type=jnp.float32)
        upward = lax.dot_general(block, uw[...], contract, preferred_element_type=jnp.float32)
        hidden = (gate * jax.nn.sigmoid(gate) * upward).astype(jnp.bfloat16)
        product = jnp.dot(hidden, dw[...], preferred_element_type=jnp.float32)
        part_b[start : start + half] = product.astype(jnp.bfloat16).reshape(half, 2, rows, width)
        for hop in range(start, start + half):
            pairs[hop] = start_send(
                part_b.at[hop, other], pair_b.at[hop], sends.at[6, hop], recvs.at[6, hop], partner
            )

    outs = []

    def forward(hop):
        pairs[hop].wait()
        both = part_b[hop, core].astype(jnp.float32) + pair_b[hop].astype(jnp.float32)
        joined_b[hop] = both.astype(jnp.bfloat16)
        outs.append(
            start_send(
                joined_b.at[hop],
                landed_b.at[hop],
                sends.at[7, hop],
                recvs.at[7, hop],
                behind[hop] * 2 + core,
            )
        )

    wait_all(passed[:half])
    feed(0)
    for hop in range(half, chips):
        take(hop)
    for hop in range(1, half):
        forward(hop)
    wait_all(passed[half:])
    feed(half)
    for hop in range(half, chips):
        forward(hop)
    pairs[0].wait()
    result = middle + part_b[0, core].astype(jnp.float32) + pair_b[0].astype(jnp.float32)
    wait_all(outs)
    for hop in range(1, chips):
        result = result + landed_b[hop].astype(jnp.float32)
    o_ref[...] = result.astype(o_ref.dtype)


def layer(attention, pick, x, out_weight, gate_weight, up_weight, down_weight, req_count, tp_count):
    rows, width = x.shape
    piece = attention.shape[2]
    chips = tp_count // 2
    most = max(req_count, tp_count)
    vmem = pl.BlockSpec(memory_space=pltpu.VMEM)
    far = pl.BlockSpec(memory_space=pl.ANY)
    gate_weight, up_weight = gate_weight.T, up_weight.T
    weights = (out_weight, gate_weight, up_weight, down_weight)
    whole = pltpu.VMEM((chips, 2, rows, width), jnp.bfloat16)
    single = pltpu.VMEM((chips, rows, width), jnp.bfloat16)
    return pl.pallas_call(
        functools.partial(layer_kernel, req_count, tp_count),
        out_shape=jax.ShapeDtypeStruct((rows, width), jnp.bfloat16),
        in_specs=[pl.BlockSpec(memory_space=pltpu.SMEM), vmem, vmem, far, far, far, far],
        out_specs=vmem,
        scratch_shapes=[
            pltpu.VMEM((tp_count, rows, piece), jnp.bfloat16),
            pltpu.VMEM((req_count * tp_count, rows, piece), jnp.bfloat16),
            whole,
            whole,
            single,
            single,
            single,
            single,
            single,
            single,
            whole,
        ]
        + [pltpu.VMEM(weight.shape, jnp.bfloat16) for weight in weights]
        + [
            pltpu.SemaphoreType.DMA((8, most)),
            pltpu.SemaphoreType.DMA((8, most)),
            pltpu.SemaphoreType.DMA((4,)),
        ],
        compiler_params=pltpu.CompilerParams(
            collective_id=1, has_side_effects=True, vmem_limit_bytes=56 * 1024 * 1024
        ),
        name="layer",
    )(pick, attention, x, *weights)


def per_device_whole(
    step_inputs,
    qkv_weight,
    qkv_bias,
    out_weight,
    gate_weight,
    up_weight,
    down_weight,
    cache_keys,
    cache_values,
    lengths,
    parents,
    slot_request,
):
    steps_count, beams, width = step_inputs.shape
    requests = slot_request.shape[0]
    req_count = lax.axis_size("req")
    tp_count = lax.axis_size("tp")
    context, kv_width = cache_keys.shape[1:]
    head_dim = kv_width // KV_HEADS
    attn_width = Q_HEADS * head_dim
    req_index = lax.axis_index("req")
    flat_index = req_index * tp_count + lax.axis_index("tp")
    rows = steps_count * beams
    key_block = min(KEY_BLOCK, context)
    request_range = jnp.arange(requests, dtype=jnp.int32)
    inverse = jnp.sum(
        jnp.where(slot_request[None, :] == request_range[:, None], request_range[None, :], 0),
        axis=1,
    )
    group_base = req_index * tp_count
    pick_slots = lax.dynamic_slice_in_dim(inverse, group_base, tp_count)
    pick_requests = lax.dynamic_slice_in_dim(slot_request, group_base, tp_count)

    mine = slot_request[flat_index]
    my_parents = lax.dynamic_index_in_dim(parents, mine, 1, keepdims=False)
    my_lengths = lax.dynamic_index_in_dim(lengths, mine, 0, keepdims=False)
    beam_range = jnp.arange(beams, dtype=jnp.int32)
    positions = []
    root_length = my_lengths
    for step in range(steps_count):
        hit = my_parents[step][:, None] == beam_range[None, :]
        root_length = jnp.sum(jnp.where(hit, root_length[None, :], 0), axis=1)
        positions.append(root_length + step)
    positions = jnp.concatenate(positions)

    inputs = step_inputs.reshape(rows, width)
    qkv = (
        jnp.dot(rms_normed(inputs), qkv_weight, preferred_element_type=jnp.float32) + qkv_bias
    ).astype(jnp.bfloat16)
    turned_width = attn_width + kv_width
    turned = rotate(qkv[:, :turned_width].reshape(rows, -1, head_dim), positions)
    packed = jnp.concatenate([turned.reshape(rows, turned_width), qkv[:, turned_width:]], axis=1)
    routed = route(packed, pick_slots, req_count, tp_count)
    routed = routed.transpose(1, 0, 2).reshape(rows, -1)

    own_parents = lax.dynamic_index_in_dim(parents, flat_index, 1, keepdims=False)
    own_lengths = lax.dynamic_index_in_dim(lengths, flat_index, 0, keepdims=False)
    plan = request_plan(own_parents, own_lengths, context, key_block)
    attention = beam_attention(
        routed[:, :attn_width].reshape(rows, Q_HEADS, head_dim),
        routed[:, attn_width:turned_width],
        routed[:, turned_width:],
        cache_keys,
        cache_values,
        plan,
        key_block,
    )
    pieces = attention.reshape(rows, tp_count, attn_width // tp_count).transpose(1, 0, 2)
    result = layer(
        pieces,
        pick_requests,
        inputs,
        out_weight,
        gate_weight,
        up_weight,
        down_weight,
        req_count,
        tp_count,
    )
    return result.reshape(steps_count, beams, width)


def per_device(*arrays):
    step_inputs, qkv_weight, cache_keys, parents = arrays[0], arrays[1], arrays[7], arrays[10]
    beams = parents.shape[2]
    tp_count = lax.axis_size("tp")
    whole = (
        step_inputs.shape[1] == beams
        and cache_keys.shape[0] == beams
        and tp_count % 4 == 0
        and qkv_weight.shape[1] % (128 * tp_count) == 0
        and cache_keys.shape[1] % min(KEY_BLOCK, cache_keys.shape[1]) == 0
    )
    return (per_device_whole if whole else per_device_split)(*arrays)


def solution(mesh):
    in_specs = (
        P(None, ("req", "tp"), None),
        P(),
        P(),
        P("tp", None),
        P(None, "tp"),
        P(None, "tp"),
        P("tp", None),
        P(("req", "tp"), None, None),
        P(("req", "tp"), None, None),
        P(),
        P(),
        P(),
    )
    out_specs = P(None, ("req", "tp"), None)
    return jax.shard_map(
        per_device, mesh=mesh, in_specs=in_specs, out_specs=out_specs, check_vma=False
    )
```

```python
import functools

import jax
import jax.numpy as jnp
from jax import lax
from jax.experimental import pallas as pl
from jax.experimental.pallas import tpu as pltpu
from jax.sharding import PartitionSpec as P

Q_HEADS = 12
KV_HEADS = 2


theta_base = 1000000.0
norm_eps = 1e-06
masked_score = -1e30


def rms_normed(values):
    values = values.astype(jnp.float32)
    factor = lax.rsqrt(jnp.mean(values * values, axis=-1, keepdims=True) + norm_eps)
    return (values * factor).astype(jnp.bfloat16)


def rotate(vectors, positions):
    half = vectors.shape[-1] // 2
    freqs = theta_base ** (-jnp.arange(half, dtype=jnp.float32) * 2.0 / vectors.shape[-1])
    angles = positions.astype(jnp.float32)[:, None] * freqs[None, :]
    cosine = jnp.cos(angles)[:, None, :]
    sine = jnp.sin(angles)[:, None, :]
    values = vectors.astype(jnp.float32)
    first = values[..., :half]
    second = values[..., half:]
    return jnp.concatenate(
        [first * cosine - second * sine, second * cosine + first * sine], axis=-1
    ).astype(jnp.bfloat16)


def owner_rows(flat, owned_count, beams, inverse):
    owned_global = flat * owned_count + jnp.arange(owned_count, dtype=jnp.int32)
    owned_request = owned_global // beams
    owned_beam = owned_global % beams
    beam_range = jnp.arange(beams, dtype=jnp.int32)
    query_rows = (inverse[owned_request][:, None] * beams + beam_range[None, :]).reshape(-1)
    return (owned_request, owned_beam, query_rows)


def owned_attention(
    every_query, keys, values, owned_request, owned_beam, query_rows, root_all, lengths
):
    owned_rows, context, kv_width = keys.shape
    beams = root_all.shape[1]
    head_dim = kv_width // KV_HEADS
    group = Q_HEADS // KV_HEADS
    grouped = jnp.take(every_query, query_rows, axis=0).reshape(
        owned_rows, beams, KV_HEADS, group, head_dim
    )
    keys = keys.reshape(owned_rows, context, KV_HEADS, head_dim)
    values = values.reshape(owned_rows, context, KV_HEADS, head_dim)
    scores = jnp.einsum(
        "jbkgd,jpkd->jbkgp", grouped, keys, preferred_element_type=jnp.float32
    ) * head_dim ** (-0.5)
    limits = lengths[owned_request, owned_beam]
    live = (jnp.arange(context, dtype=jnp.int32)[None, :] < limits[:, None])[:, None, None, None, :]
    scores = jnp.where(live, scores, masked_score)
    peak = jnp.max(scores, axis=-1)
    weights = jnp.where(live, jnp.exp(scores - peak[..., None]), 0.0)
    total = jnp.sum(weights, axis=-1)
    output = jnp.einsum(
        "jbkgp,jpkd->jbkgd",
        weights.astype(jnp.bfloat16),
        values,
        preferred_element_type=jnp.float32,
    )
    chosen = (root_all[owned_request] == owned_beam[:, None])[:, :, None, None]
    peak = jnp.where(chosen, peak, 0.0).reshape(owned_rows * beams, KV_HEADS, group)
    total = jnp.where(chosen, total, 0.0).reshape(owned_rows * beams, KV_HEADS, group)
    output = jnp.where(chosen[..., None], output, 0.0).reshape(
        owned_rows * beams, KV_HEADS, group, head_dim
    )
    return (peak, total, output)


def spread_rows(pieces, target_rows, row_count):
    return tuple(
        (
            jnp.zeros((row_count,) + piece.shape[1:], jnp.float32).at[target_rows].add(piece)
            for piece in pieces
        )
    )


def per_device_split(
    step_inputs,
    qkv_weight,
    qkv_bias,
    out_weight,
    gate_weight,
    up_weight,
    down_weight,
    cache_keys,
    cache_values,
    lengths,
    parents,
    slot_request,
):
    steps_count, rows_dev, width = step_inputs.shape
    beams = parents.shape[2]
    requests = slot_request.shape[0]
    req_count = lax.axis_size("req")
    tp_count = lax.axis_size("tp")
    group_requests = requests // req_count
    group_rows = group_requests * beams
    total_rows = requests * beams
    owned_count = cache_keys.shape[0]
    kv_width = cache_keys.shape[2]
    head_dim = kv_width // KV_HEADS
    group = Q_HEADS // KV_HEADS
    attn_width = Q_HEADS * head_dim
    req_index = lax.axis_index("req")
    tp_index = lax.axis_index("tp")
    flat_index = req_index * tp_count + tp_index
    my_requests = lax.dynamic_slice_in_dim(slot_request, req_index * group_requests, group_requests)
    inverse = (
        jnp.zeros((requests,), jnp.int32)
        .at[slot_request]
        .set(jnp.arange(requests, dtype=jnp.int32))
    )
    owned_request, owned_beam, query_rows = owner_rows(flat_index, owned_count, beams, inverse)
    beam_range = jnp.arange(beams, dtype=jnp.int32)
    root_all = jnp.broadcast_to(beam_range[None, :], (requests, beams))
    gen_keys = jnp.zeros((steps_count, group_rows, kv_width), jnp.bfloat16)
    gen_values = jnp.zeros((steps_count, group_rows, kv_width), jnp.bfloat16)
    base_rows = (jnp.arange(group_requests, dtype=jnp.int32) * beams)[:, None]
    column_width = out_weight.shape[0]
    results = []
    for step in range(steps_count):
        root_all = jnp.take_along_axis(root_all, parents[step], axis=1)
        reorder = (base_rows + parents[step][my_requests]).reshape(-1)
        gen_keys = jnp.take(gen_keys, reorder, axis=1)
        gen_values = jnp.take(gen_values, reorder, axis=1)
        inputs = step_inputs[step]
        normed = rms_normed(inputs)
        qkv = (
            jnp.dot(
                lax.all_gather(normed, "tp", axis=0, tiled=True),
                qkv_weight,
                preferred_element_type=jnp.float32,
            )
            + qkv_bias
        ).astype(jnp.bfloat16)
        my_roots = root_all[my_requests]
        positions = (jnp.take_along_axis(lengths[my_requests], my_roots, axis=1) + step).reshape(-1)
        queries = rotate(qkv[:, :attn_width].reshape(group_rows, Q_HEADS, head_dim), positions)
        new_keys = rotate(
            qkv[:, attn_width : attn_width + kv_width].reshape(group_rows, KV_HEADS, head_dim),
            positions,
        )
        gen_keys = gen_keys.at[step].set(new_keys.reshape(group_rows, kv_width))
        gen_values = gen_values.at[step].set(qkv[:, attn_width + kv_width :])
        every_query = lax.all_gather(
            queries.reshape(group_rows, attn_width), "req", axis=0, tiled=True
        )
        part_peak, part_total, part_output = owned_attention(
            every_query,
            cache_keys,
            cache_values,
            owned_request,
            owned_beam,
            query_rows,
            root_all,
            lengths,
        )
        all_peak, all_total, all_output = spread_rows(
            (part_peak, part_total, part_output), query_rows, total_rows
        )
        sum_peak, sum_total, sum_output = lax.psum((all_peak, all_total, all_output), ("req", "tp"))
        peak = lax.dynamic_slice_in_dim(sum_peak, req_index * group_rows, group_rows, 0)
        total = lax.dynamic_slice_in_dim(sum_total, req_index * group_rows, group_rows, 0)
        output = lax.dynamic_slice_in_dim(sum_output, req_index * group_rows, group_rows, 0)
        grouped = queries.reshape(group_rows, KV_HEADS, group, head_dim)
        past_keys = gen_keys[: step + 1].reshape(step + 1, group_rows, KV_HEADS, head_dim)
        past_values = gen_values[: step + 1].reshape(step + 1, group_rows, KV_HEADS, head_dim)
        recent_scores = jnp.einsum(
            "bkgd,sbkd->bkgs", grouped, past_keys, preferred_element_type=jnp.float32
        ) * head_dim ** (-0.5)
        top = jnp.maximum(peak, jnp.max(recent_scores, axis=-1))
        factor = jnp.exp(peak - top)
        recent_weights = jnp.exp(recent_scores - top[..., None])
        denominator = total * factor + jnp.sum(recent_weights, axis=-1)
        numerator = output * factor[..., None] + jnp.einsum(
            "bkgs,sbkd->bkgd",
            recent_weights.astype(jnp.bfloat16),
            past_values,
            preferred_element_type=jnp.float32,
        )
        attention = (
            (numerator / denominator[..., None])
            .reshape(group_rows, attn_width)
            .astype(jnp.bfloat16)
        )
        columns = lax.dynamic_slice_in_dim(attention, tp_index * column_width, column_width, 1)
        attended = lax.psum_scatter(
            jnp.dot(columns, out_weight, preferred_element_type=jnp.float32).astype(jnp.bfloat16),
            "tp",
            scatter_dimension=0,
            tiled=True,
        ).astype(jnp.float32)
        middle = inputs.astype(jnp.float32) + attended
        mixed_in = rms_normed(middle)
        piece = lax.all_gather(mixed_in, "tp", axis=0, tiled=True)
        gate = jnp.dot(piece, gate_weight, preferred_element_type=jnp.float32)
        upward = jnp.dot(piece, up_weight, preferred_element_type=jnp.float32)
        hidden = (jax.nn.silu(gate) * upward).astype(jnp.bfloat16)
        lowered = lax.psum_scatter(
            jnp.dot(hidden, down_weight, preferred_element_type=jnp.float32).astype(jnp.bfloat16),
            "tp",
            scatter_dimension=0,
            tiled=True,
        ).astype(jnp.float32)
        results.append((middle + lowered).astype(jnp.bfloat16))
    return jnp.stack(results)

MESH = pl.DeviceIdType.MESH
SMALL = 4
CHUNK = 8
KEY_BLOCK = 2048
HEAD_ROWS = 16


def greet(axes):
    barrier = pltpu.get_barrier_semaphore()
    total = 0
    for axis, count in axes:
        me = lax.axis_index(axis)
        for hop in range(1, count):
            peer = lax.rem(me + hop, count)
            pl.semaphore_signal(barrier, inc=1, device_id={axis: peer}, device_id_type=MESH)
        total += count - 1
    pl.semaphore_wait(barrier, total)


def start_exchange(axis, count, source, target, send_sem, recv_sem):
    me = lax.axis_index(axis)
    copies = []
    for hop in range(1, count):
        peer = lax.rem(me + hop, count)
        copy = pltpu.make_async_remote_copy(
            src_ref=source(peer),
            dst_ref=target(me),
            send_sem=send_sem.at[hop - 1],
            recv_sem=recv_sem.at[hop - 1],
            device_id={axis: peer},
            device_id_type=MESH,
        )
        copy.start()
        copies.append(copy)
    return copies


def wait_all(copies):
    for copy in copies:
        copy.wait()


def route_kernel(
    req_count, tp_count, pick_ref, x_ref, o_ref, first, second, staged, sends, recvs
):
    req_me = lax.axis_index("req")
    tp_me = lax.axis_index("tp")
    piece = x_ref.shape[1] // tp_count
    greet((("tp", tp_count), ("req", req_count)))

    def columns(peer):
        return x_ref.at[:, pl.ds(pl.multiple_of(peer * piece, piece), piece)]

    copies = start_exchange(
        "tp", tp_count, columns, lambda me: first.at[me], sends.at[0], recvs.at[0]
    )
    first[tp_me] = x_ref[:, pl.ds(pl.multiple_of(tp_me * piece, piece), piece)]
    wait_all(copies)
    group = pl.ds(req_me * tp_count, tp_count)
    copies = start_exchange(
        "req", req_count, lambda peer: first, lambda me: second.at[group], sends.at[1], recvs.at[1]
    )
    second[group] = first[...]
    wait_all(copies)
    for target in range(tp_count):
        staged[target] = second[pick_ref[target]]
    copies = start_exchange(
        "tp",
        tp_count,
        lambda peer: staged.at[peer],
        lambda me: o_ref.at[me],
        sends.at[2],
        recvs.at[2],
    )
    o_ref[tp_me] = staged[tp_me]
    wait_all(copies)


def route(x, pick, req_count, tp_count):
    rows, width = x.shape
    piece = width // tp_count
    most = max(req_count, tp_count)
    return pl.pallas_call(
        functools.partial(route_kernel, req_count, tp_count),
        out_shape=jax.ShapeDtypeStruct((tp_count, rows, piece), x.dtype),
        in_specs=[
            pl.BlockSpec(memory_space=pltpu.SMEM),
            pl.BlockSpec(memory_space=pltpu.VMEM),
        ],
        out_specs=pl.BlockSpec(memory_space=pltpu.VMEM),
        scratch_shapes=[
            pltpu.VMEM((tp_count, rows, piece), x.dtype),
            pltpu.VMEM((req_count * tp_count, rows, piece), x.dtype),
            pltpu.VMEM((tp_count, rows, piece), x.dtype),
            pltpu.SemaphoreType.DMA((3, most)),
            pltpu.SemaphoreType.DMA((3, most)),
        ],
        compiler_params=pltpu.CompilerParams(
            collective_id=0, has_side_effects=True, vmem_limit_bytes=32 * 1024 * 1024
        ),
        name="route",
    )(pick, x)


def attention_kernel(
    pairs,
    order_ref,
    begin_ref,
    count_ref,
    limit_ref,
    beam_ref,
    block_ref,
    total_ref,
    q_ref,
    kn_ref,
    vn_ref,
    seen_ref,
    k_ref,
    v_ref,
    o_ref,
    qs,
    top_s,
    sum_s,
    acc_s,
):
    item = pl.program_id(0)
    head_dim = o_ref.shape[-1]
    width = q_ref.shape[-1]
    scale = head_dim ** (-0.5)
    contract = (((1,), (1,)), ((), ()))
    key_block = k_ref.shape[0]

    @pl.when(item == 0)
    def _():
        for place in range(pairs):
            qs[place] = q_ref[order_ref[place]]
        qs[pairs:] = jnp.zeros((CHUNK,) + qs.shape[1:], qs.dtype)
        rows = pairs * HEAD_ROWS
        scores = scale * lax.dot_general(
            qs[:pairs].reshape(rows, width),
            kn_ref[...],
            contract,
            preferred_element_type=jnp.float32,
        )
        seen = seen_ref[...] > 0.5
        scores = jnp.where(seen, scores, masked_score)
        top = jnp.max(scores, axis=1, keepdims=True)
        weights = jnp.where(seen, jnp.exp(scores - top), 0.0)
        total = jnp.sum(weights, axis=1, keepdims=True)
        mixed = jnp.dot(
            weights.astype(jnp.bfloat16), vn_ref[...], preferred_element_type=jnp.float32
        )
        top_s[:pairs] = jnp.broadcast_to(top, (rows, 128)).reshape(pairs, HEAD_ROWS, 128)
        sum_s[:pairs] = jnp.broadcast_to(total, (rows, 128)).reshape(pairs, HEAD_ROWS, 128)
        acc_s[:pairs] = mixed.reshape(pairs, HEAD_ROWS, width)
        top_s[pairs:] = jnp.zeros((CHUNK, HEAD_ROWS, 128), jnp.float32)
        sum_s[pairs:] = jnp.zeros((CHUNK, HEAD_ROWS, 128), jnp.float32)
        acc_s[pairs:] = jnp.zeros((CHUNK, HEAD_ROWS, width), jnp.float32)

    @pl.when(item < total_ref[0])
    def _():
        beam = beam_ref[item]
        begin = begin_ref[beam]
        end = begin + count_ref[beam]
        left = limit_ref[beam] - block_ref[item] * key_block
        def one_chunk(base, size, keys):
            rows = size * HEAD_ROWS
            span = pl.ds(base, size)
            scores = scale * lax.dot_general(
                qs[span].reshape(rows, width),
                k_ref[:keys],
                contract,
                preferred_element_type=jnp.float32,
            )
            place = lax.broadcasted_iota(jnp.int32, (rows, keys), 1)
            row = lax.broadcasted_iota(jnp.int32, (rows, 1), 0)
            live = place < jnp.where(row < (end - base) * HEAD_ROWS, left, 0)
            scores = jnp.where(live, scores, masked_score)
            old = top_s[span].reshape(rows, 128)[:, :1]
            top = jnp.maximum(old, jnp.max(scores, axis=1, keepdims=True))
            weights = jnp.exp(scores - top)
            fade = jnp.exp(old - top)
            total = sum_s[span].reshape(rows, 128)[:, :1] * fade
            total = total + jnp.sum(weights, axis=1, keepdims=True)
            mixed = acc_s[span].reshape(rows, width) * fade + jnp.dot(
                weights.astype(jnp.bfloat16), v_ref[:keys], preferred_element_type=jnp.float32
            )
            top_s[span] = jnp.broadcast_to(top, (rows, 128)).reshape(size, HEAD_ROWS, 128)
            sum_s[span] = jnp.broadcast_to(total, (rows, 128)).reshape(size, HEAD_ROWS, 128)
            acc_s[span] = mixed.reshape(size, HEAD_ROWS, width)

        large = lax.div(end - begin + CHUNK - SMALL - 1, CHUNK)

        rest = begin + large * CHUNK

        def all_chunks(keys):
            def large_chunk(index, carry):
                one_chunk(begin + index * CHUNK, CHUNK, keys)
                return carry

            lax.fori_loop(0, large, large_chunk, 0)

            @pl.when(rest < end)
            def _():
                one_chunk(rest, SMALL, keys)

        @pl.when(left > key_block // 2)
        def _():
            all_chunks(key_block)

        @pl.when(left <= key_block // 2)
        def _():
            all_chunks(key_block // 2)

    @pl.when(item == pl.num_programs(0) - 1)
    def _():
        row = lax.broadcasted_iota(jnp.int32, (HEAD_ROWS, head_dim), 0)
        for place in range(pairs):
            mixed = acc_s[place] / sum_s[place][:, :1]
            own = jnp.where(
                row < Q_HEADS // KV_HEADS, mixed[:, :head_dim], mixed[:, head_dim:]
            )
            o_ref[order_ref[place]] = own.astype(o_ref.dtype)


def request_plan(parents, lengths, context, key_block):
    steps_count, beams = parents.shape
    beam_range = jnp.arange(beams, dtype=jnp.int32)
    pairs = steps_count * beams

    def follow(before, step):
        hit = parents[step][:, None] == beam_range[None, :]
        return jnp.sum(jnp.where(hit, before[None, :], 0), axis=1)

    root = beam_range
    roots = []
    live_from = []
    seen = []
    for step in range(steps_count):
        root = follow(root, step)
        roots.append(root)
        live_from = [follow(before, step) for before in live_from] + [beam_range]
        blocks = [
            (before[:, None] == beam_range[None, :]).astype(jnp.float32) for before in live_from
        ]
        blocks += [jnp.zeros((beams, beams), jnp.float32)] * (steps_count - step - 1)
        seen.append(jnp.concatenate(blocks, axis=1))
    seen = jnp.concatenate(seen, axis=0)
    flat = jnp.concatenate(roots)
    index = jnp.arange(pairs, dtype=jnp.int32)
    before = (flat[None, :] < flat[:, None]) | (
        (flat[None, :] == flat[:, None]) & (index[None, :] < index[:, None])
    )
    rank = jnp.sum(before.astype(jnp.int32), axis=1)
    hit = rank[None, :] == index[:, None]
    order = jnp.sum(jnp.where(hit, index[None, :], 0), axis=1)
    seen = jnp.sum(jnp.where(hit[:, :, None], seen[None], 0.0), axis=1)
    seen = jnp.repeat(seen, HEAD_ROWS, axis=0)
    begin = jnp.sum((flat[None, :] < beam_range[:, None]).astype(jnp.int32), axis=1)
    count = jnp.sum((flat[None, :] == beam_range[:, None]).astype(jnp.int32), axis=1)
    per_beam = context // key_block
    items = jnp.arange(beams * per_beam, dtype=jnp.int32)
    first = jnp.arange(per_beam, dtype=jnp.int32) * key_block
    valid = ((count > 0)[:, None] & (first[None, :] < lengths[:, None])).reshape(-1)
    total = jnp.sum(valid.astype(jnp.int32))
    ahead = jnp.sum(
        (valid[None, :] & (items[None, :] < items[:, None])).astype(jnp.int32), axis=1
    )
    wanted = jnp.minimum(items, total - 1)
    chosen = valid[None, :] & (ahead[None, :] == wanted[:, None])
    chosen = jnp.sum(jnp.where(chosen, items[None, :], 0), axis=1)
    return (
        order,
        begin,
        count,
        lengths,
        chosen // per_beam,
        chosen % per_beam,
        total.reshape(1),
        seen,
    )


def beam_attention(queries, new_keys, new_values, cache_keys, cache_values, plan, key_block):
    pairs, heads, head_dim = queries.shape
    beams, context, width = cache_keys.shape
    group = heads // KV_HEADS
    scalars, seen = plan[:-1], plan[-1]
    zero = jnp.zeros((pairs, group, head_dim), queries.dtype)
    spread = jnp.concatenate(
        [
            jnp.concatenate([queries[:, :group], zero], axis=2),
            jnp.concatenate([zero, queries[:, group:]], axis=2),
            jnp.zeros((pairs, HEAD_ROWS - heads, width), queries.dtype),
        ],
        axis=1,
    )

    def whole(shape):
        return pl.BlockSpec(shape, lambda i, *refs: (0,) * len(shape))

    def cached(i, order, begin, count, limit, beam, block, total):
        return (beam[i], block[i], 0)

    items = scalars[4].shape[0]
    return pl.pallas_call(
        functools.partial(attention_kernel, pairs),
        out_shape=jax.ShapeDtypeStruct((pairs, HEAD_ROWS, head_dim), jnp.bfloat16),
        grid_spec=pltpu.PrefetchScalarGridSpec(
            num_scalar_prefetch=7,
            grid=(items,),
            in_specs=[
                whole(spread.shape),
                whole(new_keys.shape),
                whole(new_values.shape),
                whole(seen.shape),
                pl.BlockSpec((None, key_block, width), cached),
                pl.BlockSpec((None, key_block, width), cached),
            ],
            out_specs=whole((pairs, HEAD_ROWS, head_dim)),
            scratch_shapes=[
                pltpu.VMEM((pairs + CHUNK, HEAD_ROWS, width), jnp.bfloat16),
                pltpu.VMEM((pairs + CHUNK, HEAD_ROWS, 128), jnp.float32),
                pltpu.VMEM((pairs + CHUNK, HEAD_ROWS, 128), jnp.float32),
                pltpu.VMEM((pairs + CHUNK, HEAD_ROWS, width), jnp.float32),
            ],
        ),
        compiler_params=pltpu.CompilerParams(vmem_limit_bytes=56 * 1024 * 1024),
        name="beam_attention",
    )(*scalars, spread, new_keys, new_values, seen, cache_keys, cache_values)[:, :heads]


def start_send(source, target, send_sem, recv_sem, peer):
    copy = pltpu.make_async_remote_copy(
        src_ref=source,
        dst_ref=target,
        send_sem=send_sem,
        recv_sem=recv_sem,
        device_id={"tp": peer},
        device_id_type=MESH,
    )
    copy.start()
    return copy


def layer_kernel(
    req_count,
    tp_count,
    pick_ref,
    att_ref,
    x_ref,
    ow_hbm,
    gw_hbm,
    uw_hbm,
    dw_hbm,
    o_ref,
    first,
    second,
    part_a,
    part_b,
    pair_a,
    pair_b,
    joined_a,
    joined_b,
    landed_a,
    landed_b,
    mixed,
    ow,
    gw,
    uw,
    dw,
    sends,
    recvs,
    load_sems,
):
    req_me = lax.axis_index("req")
    tp_me = lax.axis_index("tp")
    chips = tp_count // 2
    chip = tp_me // 2
    core = lax.rem(tp_me, 2)
    other = 1 - core
    partner = chip * 2 + other
    rows, width = x_ref.shape
    weights = ((ow_hbm, ow), (gw_hbm, gw), (uw_hbm, uw), (dw_hbm, dw))
    loads = [
        pltpu.make_async_copy(far, near, load_sems.at[index])
        for index, (far, near) in enumerate(weights)
    ]
    for load in loads:
        load.start()
    greet((("tp", tp_count), ("req", req_count)))
    copies = start_exchange(
        "tp",
        tp_count,
        lambda peer: att_ref.at[peer],
        lambda me: first.at[me],
        sends.at[0],
        recvs.at[0],
    )
    first[tp_me] = att_ref[tp_me]
    wait_all(copies)
    group = pl.ds(req_me * tp_count, tp_count)
    copies = start_exchange(
        "req", req_count, lambda peer: first, lambda me: second.at[group], sends.at[1], recvs.at[1]
    )
    second[group] = first[...]
    wait_all(copies)
    loads[0].wait()
    behind = [lax.rem(chip - hop + chips, chips) for hop in range(chips)]
    ahead = [lax.rem(chip + hop, chips) for hop in range(chips)]
    far_first = list(range(1, chips)) + [0]

    pairs = {}
    for hop in far_first:
        picked = jnp.concatenate(
            [second[pick_ref[behind[hop] * 2 + side]] for side in range(2)], axis=0
        )
        product = jnp.dot(picked, ow[...], preferred_element_type=jnp.float32)
        part_a[hop] = product.astype(jnp.bfloat16).reshape(2, rows, width)
        pairs[hop] = start_send(
            part_a.at[hop, other], pair_a.at[hop], sends.at[2, hop], recvs.at[2, hop], partner
        )
    outs = []
    for hop in far_first:
        pairs[hop].wait()
        both = part_a[hop, core].astype(jnp.float32) + pair_a[hop].astype(jnp.float32)
        if hop:
            joined_a[hop] = both.astype(jnp.bfloat16)
            outs.append(
                start_send(
                    joined_a.at[hop],
                    landed_a.at[hop],
                    sends.at[3, hop],
                    recvs.at[3, hop],
                    behind[hop] * 2 + core,
                )
            )
    wait_all(outs)
    middle = x_ref[...].astype(jnp.float32) + both
    for hop in range(1, chips):
        middle = middle + landed_a[hop].astype(jnp.float32)
    factor = lax.rsqrt(jnp.mean(middle * middle, axis=-1, keepdims=True) + norm_eps)
    mixed[0, core] = (middle * factor).astype(jnp.bfloat16)
    direct = {}
    for hop in range(1, chips):
        direct[hop] = start_send(
            mixed.at[0, core],
            mixed.at[hop, core],
            sends.at[4, hop],
            recvs.at[4, hop],
            ahead[hop] * 2 + core,
        )
    passed = [
        start_send(
            mixed.at[0, core], mixed.at[0, core], sends.at[5, 0], recvs.at[5, 0], partner
        )
    ]

    def take(hop):
        direct[hop].wait()
        passed.append(
            start_send(
                mixed.at[hop, core],
                mixed.at[hop, core],
                sends.at[5, hop],
                recvs.at[5, hop],
                partner,
            )
        )

    half = chips // 2
    for hop in range(1, half):
        take(hop)
    for load in loads[1:]:
        load.wait()
    contract = (((1,), (1,)), ((), ()))
    pairs = {}

    def feed(start):
        block = mixed[start : start + half].reshape(half * 2 * rows, width)
        gate = lax.dot_general(block, gw[...], contract, preferred_element_type=jnp.float32)
        upward = lax.dot_general(block, uw[...], contract, preferred_element_type=jnp.float32)
        hidden = (gate * jax.nn.sigmoid(gate) * upward).astype(jnp.bfloat16)
        product = jnp.dot(hidden, dw[...], preferred_element_type=jnp.float32)
        part_b[start : start + half] = product.astype(jnp.bfloat16).reshape(half, 2, rows, width)
        for hop in range(start, start + half):
            pairs[hop] = start_send(
                part_b.at[hop, other], pair_b.at[hop], sends.at[6, hop], recvs.at[6, hop], partner
            )

    outs = []

    def forward(hop):
        pairs[hop].wait()
        both = part_b[hop, core].astype(jnp.float32) + pair_b[hop].astype(jnp.float32)
        joined_b[hop] = both.astype(jnp.bfloat16)
        outs.append(
            start_send(
                joined_b.at[hop],
                landed_b.at[hop],
                sends.at[7, hop],
                recvs.at[7, hop],
                behind[hop] * 2 + core,
            )
        )

    wait_all(passed[:half])
    feed(0)
    for hop in range(half, chips):
        take(hop)
    for hop in range(1, half):
        forward(hop)
    wait_all(passed[half:])
    feed(half)
    for hop in range(half, chips):
        forward(hop)
    pairs[0].wait()
    result = middle + part_b[0, core].astype(jnp.float32) + pair_b[0].astype(jnp.float32)
    wait_all(outs)
    for hop in range(1, chips):
        result = result + landed_b[hop].astype(jnp.float32)
    o_ref[...] = result.astype(o_ref.dtype)


def layer(attention, pick, x, out_weight, gate_weight, up_weight, down_weight, req_count, tp_count):
    rows, width = x.shape
    piece = attention.shape[2]
    chips = tp_count // 2
    most = max(req_count, tp_count)
    vmem = pl.BlockSpec(memory_space=pltpu.VMEM)
    far = pl.BlockSpec(memory_space=pl.ANY)
    gate_weight, up_weight = gate_weight.T, up_weight.T
    weights = (out_weight, gate_weight, up_weight, down_weight)
    whole = pltpu.VMEM((chips, 2, rows, width), jnp.bfloat16)
    single = pltpu.VMEM((chips, rows, width), jnp.bfloat16)
    return pl.pallas_call(
        functools.partial(layer_kernel, req_count, tp_count),
        out_shape=jax.ShapeDtypeStruct((rows, width), jnp.bfloat16),
        in_specs=[pl.BlockSpec(memory_space=pltpu.SMEM), vmem, vmem, far, far, far, far],
        out_specs=vmem,
        scratch_shapes=[
            pltpu.VMEM((tp_count, rows, piece), jnp.bfloat16),
            pltpu.VMEM((req_count * tp_count, rows, piece), jnp.bfloat16),
            whole,
            whole,
            single,
            single,
            single,
            single,
            single,
            single,
            whole,
        ]
        + [pltpu.VMEM(weight.shape, jnp.bfloat16) for weight in weights]
        + [
            pltpu.SemaphoreType.DMA((8, most)),
            pltpu.SemaphoreType.DMA((8, most)),
            pltpu.SemaphoreType.DMA((4,)),
        ],
        compiler_params=pltpu.CompilerParams(
            collective_id=1, has_side_effects=True, vmem_limit_bytes=56 * 1024 * 1024
        ),
        name="layer",
    )(pick, attention, x, *weights)


def per_device_whole(
    step_inputs,
    qkv_weight,
    qkv_bias,
    out_weight,
    gate_weight,
    up_weight,
    down_weight,
    cache_keys,
    cache_values,
    lengths,
    parents,
    slot_request,
):
    steps_count, beams, width = step_inputs.shape
    requests = slot_request.shape[0]
    req_count = lax.axis_size("req")
    tp_count = lax.axis_size("tp")
    context, kv_width = cache_keys.shape[1:]
    head_dim = kv_width // KV_HEADS
    attn_width = Q_HEADS * head_dim
    req_index = lax.axis_index("req")
    flat_index = req_index * tp_count + lax.axis_index("tp")
    rows = steps_count * beams
    key_block = min(KEY_BLOCK, context)
    request_range = jnp.arange(requests, dtype=jnp.int32)
    inverse = jnp.sum(
        jnp.where(slot_request[None, :] == request_range[:, None], request_range[None, :], 0),
        axis=1,
    )
    group_base = req_index * tp_count
    pick_slots = lax.dynamic_slice_in_dim(inverse, group_base, tp_count)
    pick_requests = lax.dynamic_slice_in_dim(slot_request, group_base, tp_count)

    mine = slot_request[flat_index]
    my_parents = lax.dynamic_index_in_dim(parents, mine, 1, keepdims=False)
    my_lengths = lax.dynamic_index_in_dim(lengths, mine, 0, keepdims=False)
    beam_range = jnp.arange(beams, dtype=jnp.int32)
    positions = []
    root_length = my_lengths
    for step in range(steps_count):
        hit = my_parents[step][:, None] == beam_range[None, :]
        root_length = jnp.sum(jnp.where(hit, root_length[None, :], 0), axis=1)
        positions.append(root_length + step)
    positions = jnp.concatenate(positions)

    inputs = step_inputs.reshape(rows, width)
    qkv = (
        jnp.dot(rms_normed(inputs), qkv_weight, preferred_element_type=jnp.float32) + qkv_bias
    ).astype(jnp.bfloat16)
    turned_width = attn_width + kv_width
    turned = rotate(qkv[:, :turned_width].reshape(rows, -1, head_dim), positions)
    packed = jnp.concatenate([turned.reshape(rows, turned_width), qkv[:, turned_width:]], axis=1)
    routed = route(packed, pick_slots, req_count, tp_count)
    routed = routed.transpose(1, 0, 2).reshape(rows, -1)

    own_parents = lax.dynamic_index_in_dim(parents, flat_index, 1, keepdims=False)
    own_lengths = lax.dynamic_index_in_dim(lengths, flat_index, 0, keepdims=False)
    plan = request_plan(own_parents, own_lengths, context, key_block)
    attention = beam_attention(
        routed[:, :attn_width].reshape(rows, Q_HEADS, head_dim),
        routed[:, attn_width:turned_width],
        routed[:, turned_width:],
        cache_keys,
        cache_values,
        plan,
        key_block,
    )
    pieces = attention.reshape(rows, tp_count, attn_width // tp_count).transpose(1, 0, 2)
    result = layer(
        pieces,
        pick_requests,
        inputs,
        out_weight,
        gate_weight,
        up_weight,
        down_weight,
        req_count,
        tp_count,
    )
    return result.reshape(steps_count, beams, width)


def per_device(*arrays):
    step_inputs, qkv_weight, cache_keys, parents = arrays[0], arrays[1], arrays[7], arrays[10]
    beams = parents.shape[2]
    tp_count = lax.axis_size("tp")
    whole = (
        step_inputs.shape[1] == beams
        and cache_keys.shape[0] == beams
        and tp_count % 4 == 0
        and qkv_weight.shape[1] % (128 * tp_count) == 0
        and cache_keys.shape[1] % min(KEY_BLOCK, cache_keys.shape[1]) == 0
    )
    return (per_device_whole if whole else per_device_split)(*arrays)


def solution(mesh):
    in_specs = (
        P(None, ("req", "tp"), None),
        P(),
        P(),
        P("tp", None),
        P(None, "tp"),
        P(None, "tp"),
        P("tp", None),
        P(("req", "tp"), None, None),
        P(("req", "tp"), None, None),
        P(),
        P(),
        P(),
    )
    out_specs = P(None, ("req", "tp"), None)
    return jax.shard_map(
        per_device, mesh=mesh, in_specs=in_specs, out_specs=out_specs, check_vma=False
    )
```
